128 devices in a mesh: dp: 8 (over x, y_lo), tensor: 16 (over y_hi, z, core).
Axes of the slice: x: 4, y: 4 (y_hi: 2, y_lo: 2; y = y_hi * 2 + y_lo), z: 4, core: 2. Of those that a mesh axis runs over, the one named last changes fastest.
Arguments:
- tokens: bfloat16 [4096, 2048], P(('dp', 'tensor')), may hold values from -6 to 6
- cotangent: bfloat16 [4096, 2048], P(('dp', 'tensor')), may hold values from -6 to 6
- w_gate: bfloat16 [16, 2048, 5632], P(None, 'dp', 'tensor'), may hold values from -0.125 to 0.125
- w_up: bfloat16 [16, 2048, 5632], P(None, 'dp', 'tensor'), may hold values from -0.125 to 0.125
- w_down: bfloat16 [16, 5632, 2048], P(None, 'tensor', 'dp'), may hold values from -0.078125 to 0.078125
- router: float32 [16, 16], replicated, may hold values from 0 to 1, as said below
Outputs:
- grad_tokens: bfloat16 [4096, 2048], P(('dp', 'tensor'))
- grad_gate: bfloat16 [16, 2048, 5632], P(None, 'dp', 'tensor')
- grad_up: bfloat16 [16, 2048, 5632], P(None, 'dp', 'tensor')
- grad_down: bfloat16 [16, 5632, 2048], P(None, 'tensor', 'dp')
- router_grad: float32 [16, 16], replicated
The draws below stay inside these ranges and needn't reach their ends.
Inputs may be any that keep to these rules, and one draw needn't show every extreme that they name: `router`: every row is positive and sums to one.
All inputs are finite; a program needn't handle non-finite values.
Results may differ from the reference program's by a relative error of at most 0.0073.
Values may be sent and summed in bfloat16 or wider, within the bound.
A program may use at most 128 MiB of HBM per device.

```python
import jax
import jax.numpy as jnp
from jax import lax

D = 2048
FF = 5632
E = 16
SEGLEN = 256
SEG = 16
TOKENS = 4096


def draw_router(key, part):
    key = jax.random.fold_in(key, 7)
    logits = 1.5 * jax.random.normal(key, (SEG, E), jnp.float32)
    weights = jnp.exp(logits)
    return weights / jnp.sum(weights, axis=1, keepdims=True)


def shard_levels(own_key, extent, cuts, smallest, largest):
    def one(dim, blocks):
        heights = jax.random.uniform(jax.random.fold_in(jax.random.fold_in(own_key, 6), dim), (blocks,), jnp.float32, smallest / len(cuts), largest / len(cuts))
        return jnp.repeat(jnp.exp(heights), extent[dim] // blocks).reshape((-1,) + (1,) * (len(extent) - dim - 1))

    factor_of = one(*cuts[0])
    for cut in cuts[1:]:
        factor_of = factor_of * one(*cut)
    return factor_of


def bell_draw(own_key, dims, deviation, limit, cuts=(), kind=jnp.bfloat16):
    array = jax.random.normal(own_key, dims, jnp.float32) * deviation
    if len(cuts) > 0:
        array = shard_levels(own_key, dims, cuts, -0.22, 0.18) * array
    return jnp.clip(array, min=-limit, max=limit).astype(kind)


def setup_inputs(seed: int = 0) -> dict:
    seeds = jax.random.split(jax.random.key(seed), 7)
    return {
        "tokens": bell_draw(seeds[0], (TOKENS, D), 1.0, 6.0, ((0, 128),)),
        "cotangent": bell_draw(seeds[1], (TOKENS, D), 1.0, 6.0, ((0, 128),)),
        "w_gate": bell_draw(seeds[2], (E, D, FF), D ** -0.5, 0.125, ((1, 8), (2, 16))),
        "w_up": bell_draw(seeds[3], (E, D, FF), D ** -0.5, 0.125, ((1, 8), (2, 16))),
        "w_down": bell_draw(seeds[4], (E, FF, D), FF ** -0.5, 0.078125, ((1, 16), (2, 8))),
        "router": draw_router(jax.random.fold_in(seeds[6], 71), 0),
    }


def merge_one(weights, coeffs):
    merged = jnp.einsum('e,edf->df', coeffs, weights.astype(jnp.float32), precision=lax.Precision.HIGHEST)
    return merged.astype(jnp.bfloat16)

def reference(tokens, cotangent, w_gate, w_up, w_down, router):
    down_t = jnp.swapaxes(w_down, 1, 2)
    x_all = tokens.reshape(SEG, SEGLEN, D)
    dy_all = cotangent.reshape(SEG, SEGLEN, D)

    def per_segment(carry, inputs):
        x, dy, coeffs = inputs
        mgate = merge_one(w_gate, coeffs)
        mup = merge_one(w_up, coeffs)
        mdown_t = merge_one(down_t, coeffs)
        g = jnp.dot(x, mgate, preferred_element_type=jnp.float32)
        u = jnp.dot(x, mup, preferred_element_type=jnp.float32)
        sig = jax.nn.sigmoid(g)
        act = g * sig
        h = (act * u).astype(jnp.bfloat16)
        dh = jnp.dot(dy, mdown_t, preferred_element_type=jnp.float32)
        dg = (dh * u * sig * (1.0 + g * (1.0 - sig))).astype(jnp.bfloat16)
        du = (dh * act).astype(jnp.bfloat16)
        pgate = jnp.dot(x.T, dg, preferred_element_type=jnp.float32).astype(jnp.bfloat16)
        pup = jnp.dot(x.T, du, preferred_element_type=jnp.float32).astype(jnp.bfloat16)
        pdown_t = jnp.dot(dy.T, h, preferred_element_type=jnp.float32).astype(jnp.bfloat16)
        dx = jnp.dot(dg, mgate.T, preferred_element_type=jnp.float32) + jnp.dot(du, mup.T, preferred_element_type=jnp.float32)
        return (carry, (dx.astype(jnp.bfloat16), jnp.stack([pgate, pup, pdown_t])))
    unused, outs = lax.scan(per_segment, jnp.float32(0.0), (x_all, dy_all, router))
    dx_all, grads = outs
    results = []
    router_grad = jnp.zeros((SEG, E), jnp.float32)
    for index, weights in enumerate([w_gate, w_up, down_t]):
        grads_f = grads[:, index].astype(jnp.float32)
        total = jnp.einsum('se,sdf->edf', router, grads_f, precision=lax.Precision.HIGHEST)
        results.append(total.astype(jnp.bfloat16))
        router_grad = router_grad + jnp.einsum('sdf,edf->se', grads_f, weights.astype(jnp.float32), precision=lax.Precision.HIGHEST)
    router_grad = router_grad / jnp.sqrt(jnp.float32(SEGLEN * FF))
    return (dx_all.reshape(TOKENS, D), results[0], results[1], jnp.swapaxes(results[2], 1, 2), router_grad)
```

```python
import functools

import jax
import jax.numpy as jnp
from jax import lax
from jax.experimental import pallas as pl
from jax.experimental.pallas import tpu as pltpu
from jax.sharding import PartitionSpec as P

FF = 5632
SEGLEN = 256
MESH = pl.DeviceIdType.MESH
F32 = jnp.float32
BF16 = jnp.bfloat16
NX = 4
NZ = 4
GROUPS = 8
SEGS = 16
EXPERTS = 16
DS = 256
FS = 352
LANES = 128
ROWS_A = 80
ROWS_B = 96
CUT_A = 48
BASE_B = 2 * ROWS_A
FULL_B = 2 * ROWS_B
BLOCK = 32
PACK = 16

ORDER = (
    ("spread", -1),
    ("a5", 1),
    ("b5", 1),
    ("forward", 0),
    ("a6", 1),
    ("b6", 1),
    ("a2", 0),
    ("b2", 0),
    ("grads", 2),
    ("a3", 0),
    ("b3", 0),
    ("d2", 2),
    ("ea", 0),
    ("eb", 0),
    ("d3", 3),
    ("d4", 3),
)
TICKS = GROUPS + 3


def nn(a, b):
    return jnp.dot(a, b, preferred_element_type=F32)


def dims(a, b, ca, cb):
    return lax.dot_general(a, b, (((ca,), (cb,)), ((), ())), preferred_element_type=F32)


def spread_coeffs(big):
    row = lax.broadcasted_iota(jnp.int32, big.shape, 0)
    col = lax.broadcasted_iota(jnp.int32, big.shape, 1)
    own = jnp.where((row % PACK) == (col % PACK), big, 0.0)
    hi = own.astype(BF16)
    lo = (own - hi.astype(F32)).astype(BF16)
    return hi, lo


def layer_kernel(
    tok, cot, big, wg_in, wu_in, wd_in,
    dx_out, rg_out, pg_out, pu_out, pd_out,
    x, wg, wu, wd, mg, mu, md, khi, klo,
    p, h, ra1, ra2a, ra2b, ra3, rb1, rb2, rb3,
    dx, dxc, dz, rz, dy, ry, fo, outs,
    gsum, ars, arc, arz, ary, ard,
    w_sem, t1_s, t1_r, t2_s, t2_r,
    a_s, a_r, b_s, b_r, d_s, d_r, f_s, f_r, pw, r_s, r_r,
):
    d = lax.axis_index("dp")
    t = lax.axis_index("tensor")
    xi, k = d // 2, d % 2
    yh, z, c = t // 8, (t // 2) % NZ, t % 2
    right = (lax.rem(xi + 1, NX) * 2 + k, t)
    left = (lax.rem(xi + 3, NX) * 2 + k, t)
    across = (xi * 2 + 1 - k, t)
    high = (d, (1 - yh) * 8 + z * 2 + c)
    twin = (d, yh * 8 + z * 2 + 1 - c)
    xp, xm, xo = lax.rem(xi + 1, NX), lax.rem(xi + 3, NX), lax.rem(xi + 2, NX)

    def along_z(o):
        return (d, yh * 8 + lax.rem(z + o, NZ) * 2 + c)

    def along_dp(o):
        return (lax.rem(d + o, GROUPS), t)

    def remote(src, dst, ss, rs, dev):
        return pltpu.make_async_remote_copy(
            src_ref=src, dst_ref=dst, send_sem=ss, recv_sem=rs, device_id=dev, device_id_type=MESH
        )

    loads = [
        pltpu.make_async_copy(src, dst, w_sem.at[i])
        for i, (src, dst) in enumerate(((wg_in, wg), (wu_in, wu), (wd_in, wd)))
    ]
    for load in loads:
        load.start()

    peers = [along_dp(o) for o in range(1, GROUPS)] + [along_z(o) for o in range(1, NZ)] + [high, twin]
    barrier = pltpu.get_barrier_semaphore()
    for peer in peers:
        pl.semaphore_signal(barrier, inc=1, device_id=peer, device_id_type=MESH)
    pl.semaphore_wait(barrier, len(peers))

    def t1_copies(o):
        dest = lax.rem(d + o, GROUPS)
        cols = pl.ds(pl.multiple_of(dest * DS, LANES), DS)
        out = []
        for i, src in enumerate((tok, cot)):
            ref = x.at[i, 2 * d + yh, z, c]
            if o == 0:
                out.append(pltpu.make_async_copy(src.at[:, cols], ref, t1_r.at[i, 0]))
            else:
                out.append(remote(src.at[:, cols], ref, t1_s.at[i, o], t1_r.at[i, o], (dest, t)))
        return out

    for o in (4, 3, 5, 2, 6, 1, 7, 0):
        for copy in t1_copies(o):
            copy.start()

    khi[...], klo[...] = spread_coeffs(big[...])

    def merge(src, dst, rows, cols):
        def step(r, carry):
            at = pl.ds(pl.multiple_of(r * PACK, PACK), PACK)
            rhs = src[:, at, :].reshape(EXPERTS * PACK, cols)
            both = nn(khi[...], rhs) + nn(klo[...], rhs)
            dst[:, at, :] = both.astype(BF16).reshape(SEGS, PACK, cols)
            return carry

        lax.fori_loop(0, rows // PACK, step, 0, unroll=4 if rows == DS else 2)

    def t2_high(q):
        ref = x.at[:, 2 * q + yh, z, c]
        return remote(ref, ref, t2_s.at[0, q], t2_r.at[0, q], high)

    def t2_z(q, o):
        ref = x.at[:, pl.ds(2 * q, 2), z, c]
        return remote(ref, ref, t2_s.at[o, q], t2_r.at[o, q], along_z(o))

    def t2_twin(q):
        ref = x.at[:, pl.ds(2 * q, 2), :, c]
        return remote(ref, ref, t2_s.at[4, q], t2_r.at[4, q], twin)

    loads[0].wait()
    merge(wg, mg, DS, FS)

    def to_high(q, carry):
        o = lax.rem(d - q + GROUPS, GROUPS)
        for i in range(2):
            ref = x.at[i, 2 * q + yh, z, c]
            pltpu.make_async_copy(ref, ref, t1_r.at[i, o]).wait()
        t2_high(q).start()
        return carry

    lax.fori_loop(0, GROUPS, to_high, 0)
    loads[1].wait()
    merge(wu, mu, DS, FS)

    def to_z(q, carry):
        t2_high(q).wait_recv()
        for o in range(1, NZ):
            t2_z(q, o).start()
        return carry

    lax.fori_loop(0, GROUPS, to_z, 0)
    loads[2].wait()
    merge(wd, md, FS, DS)

    mine_a = pl.ds(pl.multiple_of(ROWS_A * k, PACK), ROWS_A)
    mine_a0 = pl.ds(pl.multiple_of(ROWS_A * k, PACK), CUT_A)
    mine_a1 = pl.ds(pl.multiple_of(ROWS_A * k + CUT_A, PACK), ROWS_A - CUT_A)
    theirs_a = pl.ds(pl.multiple_of(ROWS_A * (1 - k), PACK), ROWS_A)
    mine_b = pl.ds(pl.multiple_of(BASE_B + ROWS_B * k, PACK), ROWS_B)
    theirs_b = pl.ds(pl.multiple_of(BASE_B + ROWS_B * (1 - k), PACK), ROWS_B)
    all_b = pl.ds(BASE_B, FULL_B)
    b0 = pl.ds(BASE_B, ROWS_B)
    b1 = pl.ds(BASE_B + ROWS_B, ROWS_B)

    def a_copies(q):
        def cp(i, src, dst, dev):
            return remote(src, dst, a_s.at[i, q], a_r.at[i, q], dev)

        same = lambda i, ref, dev: cp(i, ref, ref, dev)
        return [
            cp(0, p.at[q, :, :, theirs_a, :], ra1.at[q], across),
            cp(1, p.at[q, xo, :, mine_a0, :], ra2a.at[q], right),
            cp(2, p.at[q, xo, :, mine_a1, :], ra2b.at[q], left),
            cp(3, p.at[q, xp, :, mine_a, :], ra3.at[q, 0], right),
            cp(4, p.at[q, xm, :, mine_a, :], ra3.at[q, 1], left),
            same(5, h.at[q, xi, :, mine_a, :], right),
            same(6, h.at[q, xi, :, mine_a, :], left),
            same(7, h.at[q, xm, :, mine_a1, :], right),
            same(8, h.at[q, xp, :, mine_a0, :], left),
            same(9, h.at[q, :, :, mine_a, :], across),
        ]

    def b_copies(q):
        def cp(i, src, dst, dev):
            return remote(src, dst, b_s.at[i, q], b_r.at[i, q], dev)

        same = lambda i, ref, dev: cp(i, ref, ref, dev)
        return [
            cp(0, p.at[q, xo, :, b0, :], rb1.at[q, 0], right),
            cp(1, p.at[q, xo, :, b1, :], rb1.at[q, 1], left),
            cp(2, p.at[q, xp, :, all_b, :], rb2.at[q, 0], right),
            cp(3, p.at[q, xm, :, all_b, :], rb2.at[q, 1], left),
            cp(4, p.at[q, xi, :, theirs_b, :], rb3.at[q], across),
            same(5, h.at[q, xi, :, mine_b, :], across),
            same(6, h.at[q, xi, :, all_b, :], right),
            same(7, h.at[q, xi, :, all_b, :], left),
            same(8, h.at[q, xm, :, b0, :], right),
            same(9, h.at[q, xp, :, b1, :], left),
        ]

    def add(ref, at, other):
        ref[at] = (ref[at].astype(F32) + other.astype(F32)).astype(BF16)

    def matrix(i, s):
        return x[i, s].reshape(SEGLEN, DS)

    def spread(q):
        for o in range(1, NZ):
            t2_z(q, o).wait_recv()
        t2_twin(q).start()

    def forward(q):
        t2_twin(q).wait_recv()
        for seg in range(2):
            s = 2 * q + seg
            xs, dys = matrix(0, s), matrix(1, s)
            for i, part in enumerate((dims(mg[s], xs, 0, 1), dims(mu[s], xs, 0, 1), dims(md[s], dys, 1, 1))):
                part = part.astype(BF16)
                for j in range(2):
                    p[q, 2 * seg + j, i] = part[:, j * LANES : (j + 1) * LANES]
        a_copies(q)[0].start()
        b_copies(q)[0].start()
        b_copies(q)[1].start()

    def a2(q):
        cps = a_copies(q)
        cps[0].wait_recv()
        add(p, (q, slice(None), slice(None), mine_a, slice(None)), ra1[q])
        cps[1].start()
        cps[2].start()

    def b2(q):
        cps = b_copies(q)
        cps[0].wait_recv()
        add(p, (q, xp, slice(None), b0, slice(None)), rb1[q, 0])
        cps[2].start()
        cps[1].wait_recv()
        add(p, (q, xm, slice(None), b1, slice(None)), rb1[q, 1])
        cps[3].start()

    def a3(q):
        cps = a_copies(q)
        cps[1].wait_recv()
        add(p, (q, xp, slice(None), mine_a0, slice(None)), ra2a[q])
        cps[3].start()
        cps[2].wait_recv()
        add(p, (q, xm, slice(None), mine_a1, slice(None)), ra2b[q])
        cps[4].start()

    def b3(q):
        cps = b_copies(q)
        cps[2].wait_recv()
        cps[3].wait_recv()
        at = (q, xi, slice(None), all_b, slice(None))
        p[at] = (p[at].astype(F32) + rb2[q, 0].astype(F32) + rb2[q, 1].astype(F32)).astype(BF16)
        cps[4].start()

    def activate(q, rows, gud):
        g, u, dh = gud
        sig = jax.nn.sigmoid(g)
        act = g * sig
        h[q, xi, 0, rows, :] = (dh * u * sig * (1.0 + g * (1.0 - sig))).astype(BF16)
        h[q, xi, 1, rows, :] = (dh * act).astype(BF16)
        h[q, xi, 2, rows, :] = (act * u).astype(BF16)

    def ea(q):
        cps = a_copies(q)
        cps[3].wait_recv()
        cps[4].wait_recv()
        activate(
            q,
            mine_a,
            [
                p[q, xi, i, mine_a, :].astype(F32) + ra3[q, 0, i].astype(F32) + ra3[q, 1, i].astype(F32)
                for i in range(3)
            ],
        )
        cps[5].start()
        cps[6].start()

    def eb(q):
        cps = b_copies(q)
        cps[4].wait_recv()
        activate(q, mine_b, [p[q, xi, i, mine_b, :].astype(F32) + rb3[q, i].astype(F32) for i in range(3)])
        cps[5].start()

    def a5(q):
        cps = a_copies(q)
        cps[5].wait_recv()
        cps[7].start()
        cps[6].wait_recv()
        cps[8].start()

    def b5(q):
        cps = b_copies(q)
        cps[5].wait_recv()
        cps[6].start()
        cps[7].start()

    def a6(q):
        cps = a_copies(q)
        cps[7].wait_recv()
        cps[8].wait_recv()
        cps[9].start()

    def b6(q):
        cps = b_copies(q)
        cps[6].wait_recv()
        cps[8].start()
        cps[7].wait_recv()
        cps[9].start()

    def keep(q):
        pair = pl.ds(2 * q, 2)
        return [
            pltpu.make_async_copy(src.at[pair], dst.at[pair], pw.at[i, q])
            for i, (src, dst) in enumerate(((mg, pg_out), (mu, pu_out), (md, pd_out)))
        ]

    def d_copies(q):
        def cp(i, src, dst, dev):
            return remote(src, dst, d_s.at[i, q], d_r.at[i, q], dev)

        return (
            [cp(0, dx.at[q, :, :, 1 - c], dxc.at[q], twin)]
            + [cp(o, dz.at[q, :, lax.rem(z + o, NZ)], rz.at[q, o - 1], along_z(o)) for o in range(1, NZ)]
            + [cp(4, dy.at[q], ry.at[q], high)]
        )

    def grads(q):
        a_copies(q)[9].wait_recv()
        b_copies(q)[8].wait_recv()
        b_copies(q)[9].wait_recv()
        parts = []
        for seg in range(2):
            s = 2 * q + seg
            dg, du, hh = (
                jnp.concatenate([h[q, 2 * seg, i], h[q, 2 * seg + 1, i]], axis=1) for i in range(3)
            )
            dxs = dims(dg, mg[s], 0, 1) + dims(du, mu[s], 0, 1)
            dx[q, seg] = dxs.reshape(NZ, 2, BLOCK, DS)
            parts.append((dg, du, hh))
        d_copies(q)[0].start()
        for seg in range(2):
            s = 2 * q + seg
            dg, du, hh = parts[seg]
            xs, dys = matrix(0, s), matrix(1, s)
            mg[s] = dims(xs, dg, 0, 1).astype(BF16)
            mu[s] = dims(xs, du, 0, 1).astype(BF16)
            md[s] = nn(hh, dys).astype(BF16)
        for copy in keep(q):
            copy.start()

    def d2(q):
        cps = d_copies(q)
        cps[0].wait_recv()
        total = dx[q, :, :, c] + dxc[q]
        dx[q, :, :, c] = total
        dz[q] = total.astype(BF16)
        for o in range(1, NZ):
            cps[o].start()

    def d3(q):
        cps = d_copies(q)
        for o in range(1, NZ):
            cps[o].wait_recv()

        def part(which):
            total = dx[q, which, z, c]
            for o in range(NZ - 1):
                total = total + rz[q, o, which].astype(F32)
            return total

        dy[q] = part(1 - yh).astype(BF16)
        cps[4].start()
        dx[q, yh, z, c] = part(yh)

    def final(q):
        o = lax.rem(q - d + GROUPS, GROUPS)
        dst = outs.at[:, pl.ds(pl.multiple_of(d * DS, LANES), DS)]
        return (
            remote(fo.at[q], dst, f_s.at[o], f_r.at[o], (q, t)),
            pltpu.make_async_copy(fo.at[q], dst, f_r.at[o]),
        )

    def d4(q):
        d_copies(q)[4].wait_recv()
        fo[q] = (dx[q, yh, z, c] + ry[q].astype(F32)).astype(BF16)
        away, stay = final(q)

        @pl.when(q != d)
        def _():
            away.start()

        @pl.when(q == d)
        def _():
            stay.start()

    stages = dict(
        spread=spread, forward=forward, a2=a2, b2=b2, a3=a3, b3=b3, ea=ea, eb=eb, a5=a5, b5=b5,
        a6=a6, b6=b6, grads=grads, d2=d2, d3=d3, d4=d4,
    )
    spread(0)

    def tick(n, carry):
        for name, lag in ORDER:
            q = n - lag

            @pl.when((q >= (1 if lag < 0 else 0)) & (q < GROUPS))
            def _(name=name, q=q):
                stages[name](q)

        return carry

    lax.fori_loop(0, TICKS, tick, 0)

    gsum[...] = jnp.zeros_like(gsum)

    def inner(grad, stacked, rows, cols):
        def step(r, carry):
            at = pl.ds(pl.multiple_of(r * PACK, PACK), PACK)
            gsum[...] += dims(
                grad[:, at, :].reshape(SEGS * PACK, cols), stacked[:, at, :].reshape(EXPERTS * PACK, cols), 1, 1
            )
            return carry

        lax.fori_loop(0, rows // PACK, step, 0, unroll=4 if rows == DS else 2)

    inner(mg, wg, DS, FS)
    inner(mu, wu, DS, FS)
    inner(md, wd, FS, DS)
    square = gsum.shape
    row = lax.broadcasted_iota(jnp.int32, square, 0)
    col = lax.broadcasted_iota(jnp.int32, square, 1)
    diag = jnp.where((row % PACK) == (col % PACK), gsum[...], 0.0)
    by_seg = jnp.sum(diag.reshape(SEGS, PACK, EXPERTS * PACK), axis=1)
    pick_row = lax.broadcasted_iota(jnp.int32, (EXPERTS * PACK, LANES), 0)
    pick_col = lax.broadcasted_iota(jnp.int32, (EXPERTS * PACK, LANES), 1)
    pick = jnp.where((pick_row // PACK) == pick_col, 1.0, 0.0).astype(F32)
    own = jnp.dot(by_seg, pick, precision=lax.Precision.HIGHEST, preferred_element_type=F32)

    def r_copies():
        def cp(i, src, dst, dev):
            return remote(src, dst, r_s.at[i], r_r.at[i], dev)

        return (
            [cp(0, ars.at[0], arc, twin)]
            + [cp(o, arz.at[z], arz.at[z], along_z(o)) for o in range(1, NZ)]
            + [cp(4, ars.at[1], ary, high)]
            + [cp(4 + o, ard.at[d], ard.at[d], along_dp(o)) for o in range(1, GROUPS)]
        )

    cps = r_copies()
    ars[0] = own
    cps[0].start()
    cps[0].wait_recv()
    arz[z] = own + arc[...]
    for o in range(1, NZ):
        cps[o].start()
    for o in range(1, NZ):
        cps[o].wait_recv()
    by_z = (arz[0] + arz[1]) + (arz[2] + arz[3])
    ars[1] = by_z
    cps[4].start()
    cps[4].wait_recv()
    ard[d] = by_z + ary[...]
    for o in range(1, GROUPS):
        cps[4 + o].start()
    for o in range(1, GROUPS):
        cps[4 + o].wait_recv()
    total = ((ard[0] + ard[1]) + (ard[2] + ard[3])) + ((ard[4] + ard[5]) + (ard[6] + ard[7]))
    rg_out[...] = total[:, :EXPERTS] / jnp.sqrt(F32(SEGLEN * FF))

    for o in range(GROUPS):
        ref = outs.at[:, pl.ds(0, DS)]
        pltpu.make_async_copy(ref, ref, f_r.at[o]).wait()
    dx_out[...] = outs[...]
    for copy in cps:
        copy.wait_send()
    for o in range(1, GROUPS):
        for copy in t1_copies(o):
            copy.wait_send()

    def drain(q, carry):
        t2_high(q).wait_send()
        for o in range(1, NZ):
            t2_z(q, o).wait_send()
        t2_twin(q).wait_send()
        for copy in a_copies(q) + b_copies(q) + d_copies(q):
            copy.wait_send()
        for copy in keep(q):
            copy.wait()

        @pl.when(q != d)
        def _():
            final(q)[0].wait_send()

        return carry

    lax.fori_loop(0, GROUPS, drain, 0)


def run_layer(tokens, cotangent, w_gate, w_up, w_down, big):
    vm, dma = pltpu.VMEM, pltpu.SemaphoreType.DMA
    any_spec = pl.BlockSpec(memory_space=pl.ANY)
    vm_spec = pl.BlockSpec(memory_space=pltpu.VMEM)
    n, half = GROUPS, FS
    scratch = [
        vm((2, SEGS, NZ, 2, BLOCK, DS), BF16),
        vm((EXPERTS, DS, FS), BF16), vm((EXPERTS, DS, FS), BF16), vm((EXPERTS, FS, DS), BF16),
        vm((SEGS, DS, FS), BF16), vm((SEGS, DS, FS), BF16), vm((SEGS, FS, DS), BF16),
        vm((DS, DS), BF16), vm((DS, DS), BF16),
        vm((n, NX, 3, FS, LANES), BF16), vm((n, NX, 3, FS, LANES), BF16),
        vm((n, NX, 3, ROWS_A, LANES), BF16),
        vm((n, 3, CUT_A, LANES), BF16), vm((n, 3, ROWS_A - CUT_A, LANES), BF16),
        vm((n, 2, 3, ROWS_A, LANES), BF16),
        vm((n, 2, 3, ROWS_B, LANES), BF16), vm((n, 2, 3, FULL_B, LANES), BF16), vm((n, 3, ROWS_B, LANES), BF16),
        vm((n, 2, NZ, 2, BLOCK, DS), F32), vm((n, 2, NZ, BLOCK, DS), F32),
        vm((n, 2, NZ, BLOCK, DS), BF16), vm((n, NZ - 1, 2, BLOCK, DS), BF16),
        vm((n, BLOCK, DS), BF16), vm((n, BLOCK, DS), BF16), vm((n, BLOCK, DS), BF16),
        vm((BLOCK, n * DS), BF16),
        vm((DS, DS), F32),
        vm((2, SEGS, LANES), F32), vm((SEGS, LANES), F32), vm((NZ, SEGS, LANES), F32),
        vm((SEGS, LANES), F32), vm((n, SEGS, LANES), F32),
        dma((3,)), dma((2, n)), dma((2, n)), dma((5, n)), dma((5, n)),
        dma((10, n)), dma((10, n)), dma((10, n)), dma((10, n)),
        dma((5, n)), dma((5, n)), dma((n,)), dma((n,)), dma((3, n)), dma((12,)), dma((12,)),
    ]
    return pl.pallas_call(
        layer_kernel,
        out_shape=(
            jax.ShapeDtypeStruct((BLOCK, n * DS), BF16),
            jax.ShapeDtypeStruct((SEGS, EXPERTS), F32),
            jax.ShapeDtypeStruct((SEGS, DS, FS), BF16),
            jax.ShapeDtypeStruct((SEGS, DS, FS), BF16),
            jax.ShapeDtypeStruct((SEGS, FS, DS), BF16),
        ),
        in_specs=[vm_spec, vm_spec, vm_spec, any_spec, any_spec, any_spec],
        out_specs=[vm_spec, vm_spec, any_spec, any_spec, any_spec],
        scratch_shapes=scratch,
        compiler_params=pltpu.CompilerParams(
            collective_id=0, has_side_effects=True, vmem_limit_bytes=63 * 2**20
        ),
        name="layer_backward",
    )(tokens, cotangent, big, w_gate, w_up, w_down)


def combine_kernel(count, big, *refs):
    srcs, dsts = refs[:count], refs[count : 2 * count]
    khi, klo = refs[2 * count :]

    @pl.when(pl.program_id(0) == 0)
    def _():
        khi[...], klo[...] = spread_coeffs(big[...])

    for src, dst in zip(srcs, dsts):
        cols = src.shape[2]
        for r in range(src.shape[1] // PACK):
            at = pl.ds(r * PACK, PACK)
            rhs = src[:, at, :].reshape(SEGS * PACK, cols)
            both = nn(khi[...], rhs) + nn(klo[...], rhs)
            dst[:, at, :] = both.astype(BF16).reshape(EXPERTS, PACK, cols)


def combine(big, rows, *parts):
    spec = lambda a: pl.BlockSpec((a.shape[0], rows, a.shape[2]), lambda i: (0, i, 0))
    return pl.pallas_call(
        functools.partial(combine_kernel, len(parts)),
        grid=(parts[0].shape[1] // rows,),
        out_shape=[jax.ShapeDtypeStruct(a.shape, BF16) for a in parts],
        in_specs=[pl.BlockSpec(memory_space=pltpu.VMEM)] + [spec(a) for a in parts],
        out_specs=[spec(a) for a in parts],
        scratch_shapes=[pltpu.VMEM((DS, DS), BF16), pltpu.VMEM((DS, DS), BF16)],
        compiler_params=pltpu.CompilerParams(vmem_limit_bytes=32 * 2**20),
        name="combine_experts",
    )(big, *parts)


def body(tokens, cotangent, w_gate, w_up, w_down, router):
    big = jnp.repeat(jnp.repeat(router, PACK, axis=0), PACK, axis=1)
    big_t = jnp.repeat(jnp.repeat(router.T, PACK, axis=0), PACK, axis=1)
    grad_tokens, router_grad, pg, pu, pd = run_layer(tokens, cotangent, w_gate, w_up, w_down, big)
    grad_gate, grad_up = combine(big_t, 32, pg, pu)
    (grad_down,) = combine(big_t, 32, pd)
    return (grad_tokens, grad_gate, grad_up, grad_down, router_grad)


def solution(mesh):
    placed = (
        P(("dp", "tensor"), None),
        P(("dp", "tensor"), None),
        P(None, "dp", "tensor"),
        P(None, "dp", "tensor"),
        P(None, "tensor", "dp"),
        P(),
    )
    return jax.shard_map(
        body,
        mesh=mesh,
        in_specs=placed,
        out_specs=(
            P(("dp", "tensor"), None),
            P(None, "dp", "tensor"),
            P(None, "dp", "tensor"),
            P(None, "tensor", "dp"),
            P(),
        ),
        check_vma=False,
    )
```

```python
import functools

import jax
import jax.numpy as jnp
from jax import lax
from jax.experimental import pallas as pl
from jax.experimental.pallas import tpu as pltpu
from jax.sharding import PartitionSpec as P

FF = 5632
SEGLEN = 256
MESH = pl.DeviceIdType.MESH
F32 = jnp.float32
BF16 = jnp.bfloat16
NX = 4
NZ = 4
NT = 16
HALVES = 2
GROUPS = 8
SEGS = 16
EXPERTS = 16
DS = 256
FS = 352
LANES = 128
ROWS_A = 80
ROWS_B = 96
CUT_A = 48
BASE_B = 2 * ROWS_A
FULL_B = 2 * ROWS_B
BLOCK = 32
PACK = 16

ORDER = (
    ("spread", -1),
    ("b3", 6),
    ("a5", 11),
    ("b2", 2),
    ("forward", 0),
    ("a3", 7),
    ("b6", 14),
    ("a6", 13),
    ("ea", 9),
    ("b5", 12),
    ("a2", 4),
    ("grads", 15),
    ("eb", 8),
    ("d2", 16),
    ("d3", 17),
    ("d4", 18),
)
LAST = 15
TAIL = tuple(name for name, lag in ORDER if lag > LAST)
TICKS = GROUPS + LAST


def nn(a, b):
    return jnp.dot(a, b, preferred_element_type=F32)


def dims(a, b, ca, cb):
    return lax.dot_general(a, b, (((ca,), (cb,)), ((), ())), preferred_element_type=F32)


def spread_coeffs(router, by_expert=False):
    wide = (SEGS * PACK, EXPERTS)
    rows = jnp.where(
        lax.broadcasted_iota(jnp.int32, wide, 0) // PACK == lax.broadcasted_iota(jnp.int32, wide, 1), 1.0, 0.0
    )
    exact = dict(precision=lax.Precision.HIGHEST, preferred_element_type=F32)
    tall = lax.dot_general(rows, router, (((1,), (int(by_expert),)), ((), ())), **exact)
    big = lax.dot_general(tall, rows, (((1,), (1,)), ((), ())), **exact)
    row = lax.broadcasted_iota(jnp.int32, big.shape, 0)
    col = lax.broadcasted_iota(jnp.int32, big.shape, 1)
    own = jnp.where((row % PACK) == (col % PACK), big, 0.0)
    hi = own.astype(BF16)
    lo = (own - hi.astype(F32)).astype(BF16)
    return hi, lo


def layer_kernel(
    tok, cot, router, wg_in, wu_in, wd_in,
    dx_out, rg_out, grad_out,
    x, w, m, khi, klo,
    p, h, ra1, ra2a, ra2b, ra3, rb1, rb2, rb3,
    dx, dxc, dz, rz, dy, ry, fo, outs,
    gsum, art, ard,
    w_sem, t1_s, t1_r, t2_s, t2_r,
    a_s, a_r, b_s, b_r, d_s, d_r, f_s, f_r, pw, r_s, r_r,
):
    d = lax.axis_index("dp")
    t = lax.axis_index("tensor")
    xi, k = d // 2, d % 2
    yh, z, c = t // 8, (t // 2) % NZ, t % 2
    right = (lax.rem(xi + 1, NX) * 2 + k, t)
    left = (lax.rem(xi + 3, NX) * 2 + k, t)
    across = (xi * 2 + 1 - k, t)
    high = (d, (1 - yh) * 8 + z * 2 + c)
    twin = (d, yh * 8 + z * 2 + 1 - c)
    xp, xm, xo = lax.rem(xi + 1, NX), lax.rem(xi + 3, NX), lax.rem(xi + 2, NX)

    def along_z(o):
        return (d, yh * 8 + lax.rem(z + o, NZ) * 2 + c)

    def along_t(o):
        return (d, lax.rem(t + o, NT))

    def along_dp(o):
        return (lax.rem(d + o, GROUPS), t)

    def remote(src, dst, ss, rs, dev):
        return pltpu.make_async_remote_copy(
            src_ref=src, dst_ref=dst, send_sem=ss, recv_sem=rs, device_id=dev, device_id_type=MESH
        )

    loads = [
        pltpu.make_async_copy(src, w.at[i], w_sem.at[i])
        for i, src in enumerate((wg_in, wu_in, wd_in))
    ]
    for load in loads:
        load.start()

    peers = [along_dp(o) for o in range(1, GROUPS)] + [along_t(o) for o in range(1, NT)]
    barrier = pltpu.get_barrier_semaphore()
    for peer in peers:
        pl.semaphore_signal(barrier, inc=1, device_id=peer, device_id_type=MESH)
    pl.semaphore_wait(barrier, len(peers))

    def t1_copies(o):
        dest = lax.rem(d + o, GROUPS)
        cols = pl.ds(pl.multiple_of(dest * DS, LANES), DS)
        out = []
        for i, src in enumerate((tok, cot)):
            ref = x.at[i, 2 * d + yh, z, c]
            if o == 0:
                out.append(pltpu.make_async_copy(src.at[:, cols], ref, t1_r.at[i, 0]))
            else:
                out.append(remote(src.at[:, cols], ref, t1_s.at[i, o], t1_r.at[i, o], (dest, t)))
        return out

    for o in (4, 3, 5, 2, 6, 1, 7, 0):
        for copy in t1_copies(o):
            copy.start()

    khi[...], klo[...] = spread_coeffs(router[...])

    def merge(i):
        def step(r, carry):
            at = pl.ds(pl.multiple_of(r * PACK, PACK), PACK)
            rhs = w[i, :, at, :].reshape(EXPERTS * PACK, DS)
            both = nn(khi[...], rhs) + nn(klo[...], rhs)
            m[i, :, at, :] = both.astype(BF16).reshape(SEGS, PACK, DS)
            return carry

        lax.fori_loop(0, FS // PACK, step, 0, unroll=11)

    def t2_high(q):
        ref = x.at[:, 2 * q + yh, z, c]
        return remote(ref, ref, t2_s.at[0, q], t2_r.at[0, q], high)

    def t2_z(q, o):
        ref = x.at[:, pl.ds(2 * q, 2), z, c]
        return remote(ref, ref, t2_s.at[o, q], t2_r.at[o, q], along_z(o))

    def t2_twin(q):
        ref = x.at[:, pl.ds(2 * q, 2), :, c]
        return remote(ref, ref, t2_s.at[4, q], t2_r.at[4, q], twin)

    loads[0].wait()
    merge(0)

    def to_high(q, carry):
        o = lax.rem(d - q + GROUPS, GROUPS)
        for i in range(2):
            ref = x.at[i, 2 * q + yh, z, c]
            pltpu.make_async_copy(ref, ref, t1_r.at[i, o]).wait()
        t2_high(q).start()
        return carry

    lax.fori_loop(0, GROUPS, to_high, 0)
    loads[1].wait()
    merge(1)

    def to_z(q, carry):
        t2_high(q).wait_recv()
        for o in range(1, NZ):
            t2_z(q, o).start()
        return carry

    lax.fori_loop(0, GROUPS, to_z, 0)
    loads[2].wait()
    merge(2)

    mine_a = pl.ds(pl.multiple_of(ROWS_A * k, PACK), ROWS_A)
    mine_a0 = pl.ds(pl.multiple_of(ROWS_A * k, PACK), CUT_A)
    mine_a1 = pl.ds(pl.multiple_of(ROWS_A * k + CUT_A, PACK), ROWS_A - CUT_A)
    theirs_a = pl.ds(pl.multiple_of(ROWS_A * (1 - k), PACK), ROWS_A)
    mine_b = pl.ds(pl.multiple_of(BASE_B + ROWS_B * k, PACK), ROWS_B)
    theirs_b = pl.ds(pl.multiple_of(BASE_B + ROWS_B * (1 - k), PACK), ROWS_B)
    all_b = pl.ds(BASE_B, FULL_B)
    b0 = pl.ds(BASE_B, ROWS_B)
    b1 = pl.ds(BASE_B + ROWS_B, ROWS_B)

    def a_copy(q, which):
        def cp(i, src, dst, dev):
            return remote(src, dst, a_s.at[i, q], a_r.at[i, q], dev)

        same = lambda i, ref, dev: cp(i, ref, ref, dev)
        return [
            lambda: cp(0, p.at[q, :, :, theirs_a, :], ra1.at[q], across),
            lambda: cp(1, p.at[q, xo, :, mine_a0, :], ra2a.at[q], right),
            lambda: cp(2, p.at[q, xo, :, mine_a1, :], ra2b.at[q], left),
            lambda: cp(3, p.at[q, xp, :, mine_a, :], ra3.at[q, 0], right),
            lambda: cp(4, p.at[q, xm, :, mine_a, :], ra3.at[q, 1], left),
            lambda: same(5, h.at[q, xi, :, mine_a, :], right),
            lambda: same(6, h.at[q, xi, :, mine_a, :], left),
            lambda: same(7, h.at[q, xm, :, mine_a1, :], right),
            lambda: same(8, h.at[q, xp, :, mine_a0, :], left),
            lambda: same(9, h.at[q, :, :, mine_a, :], across),
        ][which]()

    def b_copy(q, which):
        def cp(i, src, dst, dev):
            return remote(src, dst, b_s.at[i, q], b_r.at[i, q], dev)

        same = lambda i, ref, dev: cp(i, ref, ref, dev)
        return [
            lambda: cp(0, p.at[q, xo, :, b0, :], rb1.at[q, 0], right),
            lambda: cp(1, p.at[q, xo, :, b1, :], rb1.at[q, 1], left),
            lambda: cp(2, p.at[q, xp, :, all_b, :], rb2.at[q, 0], right),
            lambda: cp(3, p.at[q, xm, :, all_b, :], rb2.at[q, 1], left),
            lambda: cp(4, p.at[q, xi, :, theirs_b, :], rb3.at[q], across),
            lambda: same(5, h.at[q, xi, :, mine_b, :], across),
            lambda: same(6, h.at[q, xi, :, all_b, :], right),
            lambda: same(7, h.at[q, xi, :, all_b, :], left),
            lambda: same(8, h.at[q, xm, :, b0, :], right),
            lambda: same(9, h.at[q, xp, :, b1, :], left),
        ][which]()

    def add(ref, at, other):
        ref[at] = (ref[at].astype(F32) + other.astype(F32)).astype(BF16)

    def matrix(i, s):
        return x[i, s].reshape(SEGLEN, DS)

    def spread(q):
        for o in range(1, NZ):
            t2_z(q, o).wait_recv()
        t2_twin(q).start()

    def forward(q):
        t2_twin(q).wait_recv()
        for seg in range(2):
            s = 2 * q + seg
            xs, dys = matrix(0, s), matrix(1, s)
            for i, rows in enumerate((xs, xs, dys)):
                part = dims(m[i, s], rows, 1, 1).astype(BF16)
                for j in range(2):
                    p[q, 2 * seg + j, i] = part[:, j * LANES : (j + 1) * LANES]
        a_copy(q, 0).start()
        b_copy(q, 0).start()
        b_copy(q, 1).start()

    def a2(q):
        cps = lambda i: a_copy(q, i)
        cps(0).wait_recv()
        add(p, (q, slice(None), slice(None), mine_a, slice(None)), ra1[q])
        cps(1).start()
        cps(2).start()

    def b2(q):
        cps = lambda i: b_copy(q, i)
        cps(0).wait_recv()
        add(p, (q, xp, slice(None), b0, slice(None)), rb1[q, 0])
        cps(2).start()
        cps(1).wait_recv()
        add(p, (q, xm, slice(None), b1, slice(None)), rb1[q, 1])
        cps(3).start()

    def a3(q):
        cps = lambda i: a_copy(q, i)
        cps(1).wait_recv()
        add(p, (q, xp, slice(None), mine_a0, slice(None)), ra2a[q])
        cps(3).start()
        cps(2).wait_recv()
        add(p, (q, xm, slice(None), mine_a1, slice(None)), ra2b[q])
        cps(4).start()

    def b3(q):
        cps = lambda i: b_copy(q, i)
        cps(2).wait_recv()
        cps(3).wait_recv()
        at = (q, xi, slice(None), all_b, slice(None))
        p[at] = (p[at].astype(F32) + rb2[q, 0].astype(F32) + rb2[q, 1].astype(F32)).astype(BF16)
        cps(4).start()

    def activate(q, rows, gud):
        g, u, dh = gud
        sig = jax.nn.sigmoid(g)
        act = g * sig
        h[q, xi, 0, rows, :] = (dh * u * sig * (1.0 + g * (1.0 - sig))).astype(BF16)
        h[q, xi, 1, rows, :] = (dh * act).astype(BF16)
        h[q, xi, 2, rows, :] = (act * u).astype(BF16)

    def ea(q):
        cps = lambda i: a_copy(q, i)
        cps(3).wait_recv()
        cps(4).wait_recv()
        activate(
            q,
            mine_a,
            [
                p[q, xi, i, mine_a, :].astype(F32) + ra3[q, 0, i].astype(F32) + ra3[q, 1, i].astype(F32)
                for i in range(3)
            ],
        )
        cps(5).start()
        cps(6).start()

    def eb(q):
        cps = lambda i: b_copy(q, i)
        cps(4).wait_recv()
        activate(q, mine_b, [p[q, xi, i, mine_b, :].astype(F32) + rb3[q, i].astype(F32) for i in range(3)])
        cps(5).start()

    def a5(q):
        cps = lambda i: a_copy(q, i)
        cps(5).wait_recv()
        cps(7).start()
        cps(6).wait_recv()
        cps(8).start()

    def b5(q):
        cps = lambda i: b_copy(q, i)
        cps(5).wait_recv()
        cps(6).start()
        cps(7).start()

    def a6(q):
        cps = lambda i: a_copy(q, i)
        cps(7).wait_recv()
        cps(8).wait_recv()
        cps(9).start()

    def b6(q):
        cps = lambda i: b_copy(q, i)
        cps(6).wait_recv()
        cps(8).start()
        cps(7).wait_recv()
        cps(9).start()

    def keep(q):
        pair = pl.ds(2 * q, 2)
        return pltpu.make_async_copy(m.at[:, pair], grad_out.at[:, pair], pw.at[q])

    def d_copy(q, i):
        def cp(src, dst, dev):
            return remote(src, dst, d_s.at[i, q], d_r.at[i, q], dev)

        if i == 0:
            return cp(dx.at[q, :, :, 1 - c], dxc.at[q], twin)
        if i == 4:
            return cp(dy.at[q], ry.at[q], high)
        return cp(dz.at[q, :, lax.rem(z + i, NZ)], rz.at[q, i - 1], along_z(i))

    def grads(q):
        a_copy(q, 9).wait_recv()
        b_copy(q, 8).wait_recv()
        b_copy(q, 9).wait_recv()
        parts = []
        for seg in range(2):
            s = 2 * q + seg
            dg, du, hh = (
                jnp.concatenate([h[q, 2 * seg, i], h[q, 2 * seg + 1, i]], axis=1) for i in range(3)
            )
            dxs = dims(dg, m[0, s], 0, 0) + dims(du, m[1, s], 0, 0)
            dx[q, seg] = dxs.reshape(NZ, 2, BLOCK, DS)
            parts.append((dg, du, hh))
        d_copy(q, 0).start()
        for seg in range(2):
            s = 2 * q + seg
            dg, du, hh = parts[seg]
            xs, dys = matrix(0, s), matrix(1, s)
            m[0, s] = nn(dg, xs).astype(BF16)
            m[1, s] = nn(du, xs).astype(BF16)
            m[2, s] = nn(hh, dys).astype(BF16)
        keep(q).start()

    def d2(q):
        cps = lambda i: d_copy(q, i)
        cps(0).wait_recv()
        total = dx[q, :, :, c] + dxc[q]
        dx[q, :, :, c] = total
        dz[q] = total.astype(BF16)
        for o in range(1, NZ):
            cps(o).start()

    def d3(q):
        cps = lambda i: d_copy(q, i)
        for o in range(1, NZ):
            cps(o).wait_recv()

        def part(which):
            total = dx[q, which, z, c]
            for o in range(NZ - 1):
                total = total + rz[q, o, which].astype(F32)
            return total

        dy[q] = part(1 - yh).astype(BF16)
        cps(4).start()
        dx[q, yh, z, c] = part(yh)

    def final(q, away):
        o = lax.rem(q - d + GROUPS, GROUPS)
        dst = outs.at[:, pl.ds(pl.multiple_of(d * DS, LANES), DS)]
        if away:
            return remote(fo.at[q], dst, f_s.at[o], f_r.at[o], (q, t))
        return pltpu.make_async_copy(fo.at[q], dst, f_r.at[o])

    def d4(q):
        d_copy(q, 4).wait_recv()
        fo[q] = (dx[q, yh, z, c] + ry[q].astype(F32)).astype(BF16)

        @pl.when(q != d)
        def _():
            final(q, True).start()

        @pl.when(q == d)
        def _():
            final(q, False).start()

    stages = dict(
        spread=spread, forward=forward, a2=a2, b2=b2, a3=a3, b3=b3, ea=ea, eb=eb, a5=a5, b5=b5,
        a6=a6, b6=b6, grads=grads, d2=d2, d3=d3, d4=d4,
    )
    spread(0)

    def tick(n, carry):
        for name, lag in ORDER:
            q = n - lag

            @pl.when((q >= (1 if lag < 0 else 0)) & (q < GROUPS))
            def _(name=name, q=q):
                stages[name](q)

        return carry

    lax.fori_loop(0, TICKS, tick, 0)

    gsum[...] = jnp.zeros_like(gsum)

    def inner(i):
        def step(r, carry):
            at = pl.ds(pl.multiple_of(r * PACK, PACK), PACK)
            gsum[...] += dims(
                m[i, :, at, :].reshape(SEGS * PACK, DS), w[i, :, at, :].reshape(EXPERTS * PACK, DS), 1, 1
            )
            return carry

        lax.fori_loop(0, FS // PACK, step, 0, unroll=11)

    inner(0)
    d2(GROUPS - 1)
    d3(GROUPS - 2)
    d4(GROUPS - 3)
    inner(1)
    d3(GROUPS - 1)
    d4(GROUPS - 2)
    inner(2)
    square = gsum.shape
    row = lax.broadcasted_iota(jnp.int32, square, 0)
    col = lax.broadcasted_iota(jnp.int32, square, 1)
    diag = jnp.where((row % PACK) == (col % PACK), gsum[...], 0.0)
    by_seg = jnp.sum(diag.reshape(SEGS, PACK, EXPERTS * PACK), axis=1)
    pick_row = lax.broadcasted_iota(jnp.int32, (EXPERTS * PACK, LANES), 0)
    pick_col = lax.broadcasted_iota(jnp.int32, (EXPERTS * PACK, LANES), 1)
    pick = jnp.where((pick_row // PACK) == pick_col, 1.0, 0.0).astype(F32)
    own = jnp.dot(by_seg, pick, precision=lax.Precision.HIGHEST, preferred_element_type=F32)

    def r_copy(i):
        def cp(ref, dev):
            return remote(ref, ref, r_s.at[i], r_r.at[i], dev)

        if i < NT:
            return cp(art.at[t], along_t(i))
        return cp(ard.at[d], along_dp(i - NT + 1))

    art[t] = own
    for o in range(1, NT):
        r_copy(o).start()
    d4(GROUPS - 1)
    for o in range(1, NT):
        r_copy(o).wait_recv()
    ard[d] = jnp.sum(art[...], axis=0)
    for o in range(1, GROUPS):
        r_copy(NT + o - 1).start()
    for o in range(1, GROUPS):
        r_copy(NT + o - 1).wait_recv()
    total = ((ard[0] + ard[1]) + (ard[2] + ard[3])) + ((ard[4] + ard[5]) + (ard[6] + ard[7]))
    rg_out[...] = total[:, :EXPERTS] / jnp.sqrt(F32(SEGLEN * FF))

    for o in range(GROUPS):
        ref = outs.at[:, pl.ds(0, DS)]
        pltpu.make_async_copy(ref, ref, f_r.at[o]).wait()
    dx_out[...] = outs[...]
    for i in range(1, NT + GROUPS - 1):
        r_copy(i).wait_send()
    for o in range(1, GROUPS):
        for copy in t1_copies(o):
            copy.wait_send()

    def drain(q, carry):
        t2_high(q).wait_send()
        for o in range(1, NZ):
            t2_z(q, o).wait_send()
        t2_twin(q).wait_send()
        for i in range(10):
            a_copy(q, i).wait_send()
            b_copy(q, i).wait_send()
        for i in range(5):
            d_copy(q, i).wait_send()
        keep(q).wait()

        @pl.when(q != d)
        def _():
            final(q, True).wait_send()

        return carry

    lax.fori_loop(0, GROUPS, drain, 0)


def run_layer(tokens, cotangent, w_gate, w_up, w_down, router):
    vm, dma = pltpu.VMEM, pltpu.SemaphoreType.DMA
    any_spec = pl.BlockSpec(memory_space=pl.ANY)
    vm_spec = pl.BlockSpec(memory_space=pltpu.VMEM)
    n = GROUPS
    stacked = (3, SEGS, FS, DS)
    scratch = [
        vm((2, SEGS, NZ, 2, BLOCK, DS), BF16),
        vm((3, EXPERTS, FS, DS), BF16), vm(stacked, BF16),
        vm((DS, DS), BF16), vm((DS, DS), BF16),
        vm((n, NX, 3, FS, LANES), BF16), vm((n, NX, 3, FS, LANES), BF16),
        vm((n, NX, 3, ROWS_A, LANES), BF16),
        vm((n, 3, CUT_A, LANES), BF16), vm((n, 3, ROWS_A - CUT_A, LANES), BF16),
        vm((n, 2, 3, ROWS_A, LANES), BF16),
        vm((n, 2, 3, ROWS_B, LANES), BF16), vm((n, 2, 3, FULL_B, LANES), BF16), vm((n, 3, ROWS_B, LANES), BF16),
        vm((n, 2, NZ, 2, BLOCK, DS), F32), vm((n, 2, NZ, BLOCK, DS), F32),
        vm((n, 2, NZ, BLOCK, DS), BF16), vm((n, NZ - 1, 2, BLOCK, DS), BF16),
        vm((n, BLOCK, DS), BF16), vm((n, BLOCK, DS), BF16), vm((n, BLOCK, DS), BF16),
        vm((BLOCK, n * DS), BF16),
        vm((DS, DS), F32),
        vm((NT, SEGS, LANES), F32), vm((n, SEGS, LANES), F32),
        dma((3,)), dma((2, n)), dma((2, n)), dma((5, n)), dma((5, n)),
        dma((10, n)), dma((10, n)), dma((10, n)), dma((10, n)),
        dma((5, n)), dma((5, n)), dma((n,)), dma((n,)), dma((n,)), dma((NT + n - 1,)), dma((NT + n - 1,)),
    ]
    return pl.pallas_call(
        layer_kernel,
        out_shape=(
            jax.ShapeDtypeStruct((BLOCK, n * DS), BF16),
            jax.ShapeDtypeStruct((SEGS, EXPERTS), F32),
            jax.ShapeDtypeStruct(stacked, BF16),
        ),
        in_specs=[vm_spec, vm_spec, vm_spec, any_spec, any_spec, any_spec],
        out_specs=[vm_spec, vm_spec, any_spec],
        scratch_shapes=scratch,
        compiler_params=pltpu.CompilerParams(
            collective_id=0, has_side_effects=True, vmem_limit_bytes=63 * 2**20
        ),
        name="layer_backward",
    )(tokens, cotangent, router, w_gate, w_up, w_down)


def combine_kernel(router, src, dx_in, rg_in, gate, up, down, dx_out, rg_out, got, made, khi, klo, in_sem, out_sem, pass_sem):
    rows = FS // HALVES
    chunks = [(i, pl.ds(j * rows, rows)) for i in range(3) for j in range(HALVES)]
    ins = [pltpu.make_async_copy(src.at[i, :, at], got.at[n], in_sem.at[n]) for n, (i, at) in enumerate(chunks)]
    outs = [
        pltpu.make_async_copy(made.at[n], (gate, up, down)[i].at[:, at], out_sem.at[n])
        for n, (i, at) in enumerate(chunks)
    ]
    passed = [
        pltpu.make_async_copy(dx_in, dx_out, pass_sem.at[0]),
        pltpu.make_async_copy(rg_in, rg_out, pass_sem.at[1]),
    ]
    for copy in ins + passed:
        copy.start()
    khi[...], klo[...] = spread_coeffs(router[...], by_expert=True)
    for n in range(len(chunks)):
        ins[n].wait()

        def step(r, carry, n=n):
            at = pl.ds(pl.multiple_of(r * PACK, PACK), PACK)
            rhs = got[n, :, at, :].reshape(SEGS * PACK, DS)
            both = nn(khi[...], rhs) + nn(klo[...], rhs)
            made[n, :, at, :] = both.astype(BF16).reshape(EXPERTS, PACK, DS)
            return carry

        lax.fori_loop(0, rows // PACK, step, 0, unroll=11)
        outs[n].start()
    for copy in outs + passed:
        copy.wait()


def combine(router, grads, grad_tokens, router_grad):
    any_spec = pl.BlockSpec(memory_space=pl.ANY)
    n = 3 * HALVES
    like = lambda a: jax.ShapeDtypeStruct(a.shape, a.dtype)
    return pl.pallas_call(
        combine_kernel,
        out_shape=[jax.ShapeDtypeStruct((EXPERTS, FS, DS), BF16)] * 3 + [like(grad_tokens), like(router_grad)],
        in_specs=[pl.BlockSpec(memory_space=pltpu.VMEM)] + [any_spec] * 3,
        out_specs=[any_spec] * 5,
        scratch_shapes=[pltpu.VMEM((n, SEGS, FS // HALVES, DS), BF16)] * 2
        + [pltpu.VMEM((DS, DS), BF16)] * 2
        + [pltpu.SemaphoreType.DMA((n,)), pltpu.SemaphoreType.DMA((n,)), pltpu.SemaphoreType.DMA((2,))],
        compiler_params=pltpu.CompilerParams(vmem_limit_bytes=60 * 2**20),
        name="combine_experts",
    )(router, grads, grad_tokens, router_grad)


def body(tokens, cotangent, w_gate, w_up, w_down, router):
    flip = lambda a: jnp.swapaxes(a, 1, 2)
    grad_tokens, router_grad, grads = run_layer(
        tokens, cotangent, flip(w_gate), flip(w_up), w_down, router
    )
    grad_gate, grad_up, grad_down, grad_tokens, router_grad = combine(router, grads, grad_tokens, router_grad)
    return (grad_tokens, flip(grad_gate), flip(grad_up), grad_down, router_grad)


def solution(mesh):
    placed = (
        P(("dp", "tensor"), None),
        P(("dp", "tensor"), None),
        P(None, "dp", "tensor"),
        P(None, "dp", "tensor"),
        P(None, "tensor", "dp"),
        P(),
    )
    return jax.shard_map(
        body,
        mesh=mesh,
        in_specs=placed,
        out_specs=(
            P(("dp", "tensor"), None),
            P(None, "dp", "tensor"),
            P(None, "dp", "tensor"),
            P(None, "tensor", "dp"),
            P(),
        ),
        check_vma=False,
    )
```

```python
import functools

import jax
import jax.numpy as jnp
from jax import lax
from jax.experimental import pallas as pl
from jax.experimental.pallas import tpu as pltpu
from jax.sharding import PartitionSpec as P

FF = 5632
SEGLEN = 256
MESH = pl.DeviceIdType.MESH
F32 = jnp.float32
BF16 = jnp.bfloat16
NX = 4
NZ = 4
NT = 16
HALVES = 2
GROUPS = 8
OWN = 4
SEGS = 16
EXPERTS = 16
DS = 256
FS = 352
LANES = 128
ROWS_A = 80
ROWS_B = 96
CUT_A = 48
BASE_B = 2 * ROWS_A
FULL_B = 2 * ROWS_B
BACK_A = 64
BACK_B = 112
SWAP = ROWS_A - BACK_A
CUT_BACK = 32
BASE_BACK = 2 * BACK_A
FULL_BACK = 2 * BACK_B
PLACES = (
    (0, 0, BACK_A),
    (BACK_A, BASE_BACK, SWAP),
    (ROWS_A, BACK_A, BACK_A),
    (ROWS_A + BACK_A, BASE_BACK + BACK_B, SWAP),
    (BASE_B, BASE_BACK + SWAP, ROWS_B),
    (BASE_B + ROWS_B, BASE_BACK + BACK_B + SWAP, ROWS_B),
)
BLOCK = 32
PACK = 16

ORDER = (
    ("spread", -1),
    ("b3", 6),
    ("a2", 3),
    ("grads", 13),
    ("forward", 0),
    ("a6", 11),
    ("a5", 10),
    ("eb", 8),
    ("b2", 1),
    ("ea", 8),
    ("b5", 10),
    ("a3", 4),
    ("b6", 11),
    ("d2", 14),
    ("d3", 15),
    ("d4", 16),
)
LAST = 13
TICKS = GROUPS + LAST


def nn(a, b):
    return jnp.dot(a, b, preferred_element_type=F32)


def dims(a, b, ca, cb):
    return lax.dot_general(a, b, (((ca,), (cb,)), ((), ())), preferred_element_type=F32)


def spread_coeffs(router, by_expert=False):
    wide = (SEGS * PACK, EXPERTS)
    rows = jnp.where(
        lax.broadcasted_iota(jnp.int32, wide, 0) // PACK == lax.broadcasted_iota(jnp.int32, wide, 1), 1.0, 0.0
    )
    exact = dict(precision=lax.Precision.HIGHEST, preferred_element_type=F32)
    tall = lax.dot_general(rows, router, (((1,), (int(by_expert),)), ((), ())), **exact)
    big = lax.dot_general(tall, rows, (((1,), (1,)), ((), ())), **exact)
    row = lax.broadcasted_iota(jnp.int32, big.shape, 0)
    col = lax.broadcasted_iota(jnp.int32, big.shape, 1)
    own = jnp.where((row % PACK) == (col % PACK), big, 0.0)
    hi = own.astype(BF16)
    lo = (own - hi.astype(F32)).astype(BF16)
    return hi, lo


def layer_kernel(
    tok_in, cot_in, router_in, wg_in, wu_in, wd_in,
    dx_out, rg_out, grad_out,
    rows_in, router, x, w, m, khi, klo,
    p, h, ra1, ra2a, ra2b, ra3, rb1, rb2, rb3,
    dx, dxc, dz, rz, dy, ry, fo, outs,
    gsum, art, ard,
    w_sem, t1_s, t1_r, t2_s, t2_r,
    a_s, a_r, b_s, b_r, d_s, d_r, f_s, f_r, pw, r_s, r_r,
):
    d = lax.axis_index("dp")
    t = lax.axis_index("tensor")
    xi, k = d // 2, d % 2
    yh, z, c = t // 8, (t // 2) % NZ, t % 2
    right = (lax.rem(xi + 1, NX) * 2 + k, t)
    left = (lax.rem(xi + 3, NX) * 2 + k, t)
    across = (xi * 2 + 1 - k, t)
    high = (d, (1 - yh) * 8 + z * 2 + c)
    twin = (d, yh * 8 + z * 2 + 1 - c)
    xp, xm, xo = lax.rem(xi + 1, NX), lax.rem(xi + 3, NX), lax.rem(xi + 2, NX)

    def along_z(o):
        return (d, yh * 8 + lax.rem(z + o, NZ) * 2 + c)

    def along_t(o):
        return (d, lax.rem(t + o, NT))

    def along_dp(o):
        return (lax.rem(d + o, GROUPS), t)

    def remote(src, dst, ss, rs, dev):
        return pltpu.make_async_remote_copy(
            src_ref=src, dst_ref=dst, send_sem=ss, recv_sem=rs, device_id=dev, device_id_type=MESH
        )

    loads = [
        pltpu.make_async_copy(src, w.at[i], w_sem.at[i])
        for i, src in enumerate((wg_in, wu_in, wd_in))
    ]
    loads += [
        pltpu.make_async_copy(tok_in, rows_in.at[0], w_sem.at[3]),
        pltpu.make_async_copy(cot_in, rows_in.at[1], w_sem.at[4]),
        pltpu.make_async_copy(router_in, router, w_sem.at[5]),
    ]
    for i in (5, 0, 3, 4, 1, 2):
        loads[i].start()

    peers = [along_dp(o) for o in range(1, GROUPS)] + [along_z(o) for o in range(1, NZ)] + [high, twin]
    barrier = pltpu.get_barrier_semaphore()
    for peer in peers:
        pl.semaphore_signal(barrier, inc=1, device_id=peer, device_id_type=MESH)

    def t1_copy(o):
        dest = lax.rem(d + o, GROUPS)
        cols = pl.ds(pl.multiple_of(dest * DS, LANES), DS)
        src, dst = rows_in.at[:, :, cols], x.at[:, d, yh, z, c]
        if o == 0:
            return pltpu.make_async_copy(src, dst, t1_r.at[0])
        return remote(src, dst, t1_s.at[o], t1_r.at[o], (dest, t))

    loads[5].wait()
    khi[...], klo[...] = spread_coeffs(router[...])

    def merge(i):
        def step(r, carry):
            at = pl.ds(pl.multiple_of(r * PACK, PACK), PACK)
            rhs = w[i, :, at, :].reshape(EXPERTS * PACK, DS)
            both = nn(khi[...], rhs) + nn(klo[...], rhs)
            m[i, :, at, :] = both.astype(BF16).reshape(SEGS, PACK, DS)
            return carry

        lax.fori_loop(0, FS // PACK, step, 0, unroll=11)

    loads[0].wait()
    merge(0)
    pl.semaphore_wait(barrier, len(peers))
    loads[3].wait()
    loads[4].wait()
    for o in (4, 3, 5, 2, 6, 1, 7, 0):
        t1_copy(o).start()
    for i in (1, 2):
        loads[i].wait()
        merge(i)

    def group(q):
        return 2 * lax.rem(q, OWN), lax.rem(yh + q // OWN, 2)

    def segment(q, i):
        first, which = group(q)
        return 2 * (first + i) + which

    def t2_high(a):
        ref = x.at[:, pl.ds(2 * a, 2), yh, z, c]
        return remote(ref, ref, t2_s.at[0, a], t2_r.at[0, a], high)

    def t2_z(q, o):
        first, which = group(q)
        ref = x.at[:, pl.ds(first, 2), which, z, c]
        return remote(ref, ref, t2_s.at[o, q], t2_r.at[o, q], along_z(o))

    def t2_twin(q):
        first, which = group(q)
        ref = x.at[:, pl.ds(first, 2), which, :, c]
        return remote(ref, ref, t2_s.at[4, q], t2_r.at[4, q], twin)

    def hand_on(a, carry):
        for i in range(2):
            o = lax.rem(d - 2 * a - i + GROUPS, GROUPS)
            ref = x.at[:, 2 * a + i, yh, z, c]
            pltpu.make_async_copy(ref, ref, t1_r.at[o]).wait()
        for o in (2, 1, 3):
            t2_z(a, o).start()
        t2_high(a).start()
        return carry

    def hand_on_other(a, carry):
        t2_high(a).wait_recv()
        for o in (2, 1, 3):
            t2_z(OWN + a, o).start()
        return carry

    lax.fori_loop(0, OWN, hand_on, 0)
    lax.fori_loop(0, OWN, hand_on_other, 0)

    mine_a = pl.ds(pl.multiple_of(ROWS_A * k, PACK), ROWS_A)
    mine_a0 = pl.ds(pl.multiple_of(ROWS_A * k, PACK), CUT_A)
    mine_a1 = pl.ds(pl.multiple_of(ROWS_A * k + CUT_A, PACK), ROWS_A - CUT_A)
    theirs_a = pl.ds(pl.multiple_of(ROWS_A * (1 - k), PACK), ROWS_A)
    mine_b = pl.ds(pl.multiple_of(BASE_B + ROWS_B * k, PACK), ROWS_B)
    theirs_b = pl.ds(pl.multiple_of(BASE_B + ROWS_B * (1 - k), PACK), ROWS_B)
    all_b = pl.ds(BASE_B, FULL_B)
    back_a = pl.ds(pl.multiple_of(BACK_A * k, PACK), BACK_A)
    back_a0 = pl.ds(pl.multiple_of(BACK_A * k, PACK), CUT_BACK)
    back_a1 = pl.ds(pl.multiple_of(BACK_A * k + CUT_BACK, PACK), BACK_A - CUT_BACK)
    swap = pl.ds(pl.multiple_of(BASE_BACK + BACK_B * k, PACK), SWAP)
    rest = pl.ds(pl.multiple_of(BASE_BACK + BACK_B * k + SWAP, PACK), ROWS_B)
    back_b = pl.ds(pl.multiple_of(BASE_BACK + BACK_B * k, PACK), BACK_B)
    all_back = pl.ds(BASE_BACK, FULL_BACK)
    back_b0 = pl.ds(BASE_BACK, BACK_B)
    back_b1 = pl.ds(BASE_BACK + BACK_B, BACK_B)
    b0 = pl.ds(BASE_B, ROWS_B)
    b1 = pl.ds(BASE_B + ROWS_B, ROWS_B)

    def a_copy(q, which):
        def cp(i, src, dst, dev):
            return remote(src, dst, a_s.at[i, q], a_r.at[i, q], dev)

        same = lambda i, ref, dev: cp(i, ref, ref, dev)
        return [
            lambda: cp(0, p.at[q, :, :, theirs_a, :], ra1.at[q], across),
            lambda: cp(1, p.at[q, xo, :, mine_a0, :], ra2a.at[q], right),
            lambda: cp(2, p.at[q, xo, :, mine_a1, :], ra2b.at[q], left),
            lambda: cp(3, p.at[q, xp, :, mine_a, :], ra3.at[q, 0], right),
            lambda: cp(4, p.at[q, xm, :, mine_a, :], ra3.at[q, 1], left),
            lambda: same(5, h.at[q, xi, :, back_a, :], right),
            lambda: same(6, h.at[q, xi, :, back_a, :], left),
            lambda: same(7, h.at[q, xm, :, back_a1, :], right),
            lambda: same(8, h.at[q, xp, :, back_a0, :], left),
            lambda: same(9, h.at[q, :, :, back_a, :], across),
        ][which]()

    def b_copy(q, which):
        def cp(i, src, dst, dev):
            return remote(src, dst, b_s.at[i, q], b_r.at[i, q], dev)

        same = lambda i, ref, dev: cp(i, ref, ref, dev)
        return [
            lambda: cp(0, p.at[q, xo, :, b0, :], rb1.at[q, 0], right),
            lambda: cp(1, p.at[q, xo, :, b1, :], rb1.at[q, 1], left),
            lambda: cp(2, p.at[q, xp, :, all_b, :], rb2.at[q, 0], right),
            lambda: cp(3, p.at[q, xm, :, all_b, :], rb2.at[q, 1], left),
            lambda: cp(4, p.at[q, xi, :, theirs_b, :], rb3.at[q], across),
            lambda: same(5, h.at[q, xi, :, back_b, :], across),
            lambda: same(6, h.at[q, xi, :, all_back, :], right),
            lambda: same(7, h.at[q, xi, :, all_back, :], left),
            lambda: same(8, h.at[q, xm, :, back_b0, :], right),
            lambda: same(9, h.at[q, xp, :, back_b1, :], left),
        ][which]()

    def add(ref, at, other):
        ref[at] = (ref[at].astype(F32) + other.astype(F32)).astype(BF16)

    def matrix(i, q, seg):
        first, which = group(q)
        return x[i, first + seg, which].reshape(SEGLEN, DS)

    def spread(q):
        for o in range(1, NZ):
            t2_z(q, o).wait_recv()
        t2_twin(q).start()

    def forward(q):
        t2_twin(q).wait_recv()
        for seg in range(2):
            s = segment(q, seg)
            xs, dys = matrix(0, q, seg), matrix(1, q, seg)
            for i, rows in enumerate((xs, xs, dys)):
                part = dims(m[i, s], rows, 1, 1).astype(BF16)
                for j in range(2):
                    half = part[:, j * LANES : (j + 1) * LANES]
                    for place, unit, count in PLACES:
                        p[q, 2 * seg + j, i, place : place + count] = half[unit : unit + count]
        a_copy(q, 0).start()
        b_copy(q, 0).start()
        b_copy(q, 1).start()

    def a2(q):
        cps = lambda i: a_copy(q, i)
        cps(0).wait_recv()
        add(p, (q, slice(None), slice(None), mine_a, slice(None)), ra1[q])
        cps(1).start()
        cps(2).start()

    def b2(q):
        cps = lambda i: b_copy(q, i)
        cps(0).wait_recv()
        add(p, (q, xp, slice(None), b0, slice(None)), rb1[q, 0])
        cps(2).start()
        cps(1).wait_recv()
        add(p, (q, xm, slice(None), b1, slice(None)), rb1[q, 1])
        cps(3).start()

    def a3(q):
        cps = lambda i: a_copy(q, i)
        cps(1).wait_recv()
        add(p, (q, xp, slice(None), mine_a0, slice(None)), ra2a[q])
        cps(3).start()
        cps(2).wait_recv()
        add(p, (q, xm, slice(None), mine_a1, slice(None)), ra2b[q])
        cps(4).start()

    def b3(q):
        cps = lambda i: b_copy(q, i)
        cps(2).wait_recv()
        cps(3).wait_recv()
        at = (q, xi, slice(None), all_b, slice(None))
        p[at] = (p[at].astype(F32) + rb2[q, 0].astype(F32) + rb2[q, 1].astype(F32)).astype(BF16)
        cps(4).start()

    def activate(q, gud, *spans):
        g, u, dh = gud
        sig = jax.nn.sigmoid(g)
        act = g * sig
        made = (dh * u * sig * (1.0 + g * (1.0 - sig)), dh * act, act * u)
        for i, part in enumerate(made):
            first = 0
            for span in spans:
                h[q, xi, i, span, :] = part[first : first + span.size].astype(BF16)
                first += span.size

    def ea(q):
        cps = lambda i: a_copy(q, i)
        cps(3).wait_recv()
        cps(4).wait_recv()
        activate(
            q,
            [
                p[q, xi, i, mine_a, :].astype(F32) + ra3[q, 0, i].astype(F32) + ra3[q, 1, i].astype(F32)
                for i in range(3)
            ],
            back_a,
            swap,
        )
        b_copy(q, 5).start()
        cps(5).start()
        cps(6).start()

    def eb(q):
        cps = lambda i: b_copy(q, i)
        cps(4).wait_recv()
        activate(q, [p[q, xi, i, mine_b, :].astype(F32) + rb3[q, i].astype(F32) for i in range(3)], rest)

    def a5(q):
        cps = lambda i: a_copy(q, i)
        cps(5).wait_recv()
        cps(7).start()
        cps(6).wait_recv()
        cps(8).start()

    def b5(q):
        cps = lambda i: b_copy(q, i)
        cps(5).wait_recv()
        cps(6).start()
        cps(7).start()

    def a6(q):
        cps = lambda i: a_copy(q, i)
        cps(7).wait_recv()
        cps(8).wait_recv()
        cps(9).start()

    def b6(q):
        cps = lambda i: b_copy(q, i)
        cps(6).wait_recv()
        cps(8).start()
        cps(7).wait_recv()
        cps(9).start()

    def keep(q, seg):
        s = segment(q, seg)
        return pltpu.make_async_copy(m.at[:, s], grad_out.at[:, s], pw.at[seg, q])

    def d_copy(q, i):
        def cp(src, dst, dev):
            return remote(src, dst, d_s.at[i, q], d_r.at[i, q], dev)

        if i == 0:
            return cp(dx.at[q, :, :, 1 - c], dxc.at[q], twin)
        if i == 4:
            return remote(dy.at[q], ry.at[q], d_s.at[i, q], d_r.at[i, q], high)
        return cp(dz.at[q, :, lax.rem(z + i, NZ)], rz.at[q, i - 1], along_z(i))

    def grads(q):
        a_copy(q, 9).wait_recv()
        b_copy(q, 8).wait_recv()
        b_copy(q, 9).wait_recv()
        parts = []
        for seg in range(2):
            s = segment(q, seg)
            dg, du, hh = (
                jnp.concatenate([h[q, 2 * seg, i], h[q, 2 * seg + 1, i]], axis=1) for i in range(3)
            )
            dxs = dims(dg, m[0, s], 0, 0) + dims(du, m[1, s], 0, 0)
            dx[q, seg] = dxs.reshape(NZ, 2, BLOCK, DS)
            parts.append((dg, du, hh))
        d_copy(q, 0).start()
        for seg in range(2):
            s = segment(q, seg)
            dg, du, hh = parts[seg]
            xs, dys = matrix(0, q, seg), matrix(1, q, seg)
            m[0, s] = nn(dg, xs).astype(BF16)
            m[1, s] = nn(du, xs).astype(BF16)
            m[2, s] = nn(hh, dys).astype(BF16)
            keep(q, seg).start()

    def d2(q):
        cps = lambda i: d_copy(q, i)
        cps(0).wait_recv()
        total = dx[q, :, :, c] + dxc[q]
        dx[q, :, :, c] = total
        dz[q] = total.astype(BF16)
        for o in range(1, NZ):
            cps(o).start()

    def d3(q):
        cps = lambda i: d_copy(q, i)
        for o in range(1, NZ):
            cps(o).wait_recv()

        total = dx[q, :, z, c]
        for o in range(NZ - 1):
            total = total + rz[q, o].astype(F32)

        @pl.when(q >= OWN)
        def _():
            dy[q - OWN] = total.astype(BF16)
            d_copy(q - OWN, 4).start()

        @pl.when(q < OWN)
        def _():
            dx[q, :, z, c] = total

    def final(dest, away):
        o = lax.rem(dest - d + GROUPS, GROUPS)
        src, dst = fo.at[dest], outs.at[:, pl.ds(pl.multiple_of(d * DS, LANES), DS)]
        if away:
            return remote(src, dst, f_s.at[o], f_r.at[o], (dest, t))
        return pltpu.make_async_copy(src, dst, f_r.at[o])

    def d4(q):
        @pl.when(q >= OWN)
        def _():
            a = q - OWN
            d_copy(a, 4).wait_recv()
            for i in range(2):
                dest = 2 * a + i
                fo[dest] = (dx[a, i, z, c] + ry[a, i].astype(F32)).astype(BF16)

                @pl.when(dest != d)
                def _(dest=dest):
                    final(dest, True).start()

                @pl.when(dest == d)
                def _(dest=dest):
                    final(dest, False).start()

    stages = dict(
        spread=spread, forward=forward, a2=a2, b2=b2, a3=a3, b3=b3, ea=ea, eb=eb, a5=a5, b5=b5,
        a6=a6, b6=b6, grads=grads, d2=d2, d3=d3, d4=d4,
    )
    spread(0)

    def tick(n, carry):
        for name, lag in ORDER:
            q = n - lag

            @pl.when((q >= (1 if lag < 0 else 0)) & (q < GROUPS))
            def _(name=name, q=q):
                stages[name](q)

        return carry

    lax.fori_loop(0, TICKS, tick, 0)

    gsum[...] = jnp.zeros_like(gsum)

    def inner(i):
        def step(r, carry):
            at = pl.ds(pl.multiple_of(r * PACK, PACK), PACK)
            gsum[...] += dims(
                m[i, :, at, :].reshape(SEGS * PACK, DS), w[i, :, at, :].reshape(EXPERTS * PACK, DS), 1, 1
            )
            return carry

        lax.fori_loop(0, FS // PACK, step, 0, unroll=11)

    last = jnp.int32(GROUPS - 1)
    inner(0)
    d2(last)
    d3(last - 1)
    d4(last - 2)
    inner(1)
    inner(2)
    square = gsum.shape
    row = lax.broadcasted_iota(jnp.int32, square, 0)
    col = lax.broadcasted_iota(jnp.int32, square, 1)
    diag = jnp.where((row % PACK) == (col % PACK), gsum[...], 0.0)
    by_seg = jnp.sum(diag.reshape(SEGS, PACK, EXPERTS * PACK), axis=1)
    pick_row = lax.broadcasted_iota(jnp.int32, (EXPERTS * PACK, LANES), 0)
    pick_col = lax.broadcasted_iota(jnp.int32, (EXPERTS * PACK, LANES), 1)
    pick = jnp.where((pick_row // PACK) == pick_col, 1.0, 0.0).astype(F32)
    own = jnp.dot(by_seg, pick, precision=lax.Precision.HIGHEST, preferred_element_type=F32)

    def r_copy(i):
        def cp(ref, dev):
            return remote(ref, ref, r_s.at[i], r_r.at[i], dev)

        if i < NT:
            return cp(art.at[t], along_t(i))
        return cp(ard.at[d], along_dp(i - NT + 1))

    art[t] = own
    for o in range(1, NT):
        r_copy(o).start()
    d3(last)
    d4(last - 1)

    def drain(q, carry):
        for i in range(10):
            a_copy(q, i).wait_send()
            b_copy(q, i).wait_send()
        return carry

    lax.fori_loop(0, GROUPS, drain, 0)
    for o in range(1, NT):
        r_copy(o).wait_recv()
    ard[d] = jnp.sum(art[...], axis=0)
    for o in range(1, GROUPS):
        r_copy(NT + o - 1).start()
    d4(last)

    def drain_rest(q, carry):
        for o in range(1, NZ):
            t2_z(q, o).wait_send()
            d_copy(q, o).wait_send()
        t2_twin(q).wait_send()
        d_copy(q, 0).wait_send()
        for seg in range(2):
            keep(q, seg).wait()

        @pl.when(q < OWN)
        def _():
            t2_high(q).wait_send()
            d_copy(q, 4).wait_send()

        return carry

    lax.fori_loop(0, GROUPS, drain_rest, 0)
    for o in range(1, GROUPS):
        t1_copy(o).wait_send()
    for o in range(1, NT):
        r_copy(o).wait_send()
    for o in range(1, GROUPS):
        r_copy(NT + o - 1).wait_recv()
    total = ((ard[0] + ard[1]) + (ard[2] + ard[3])) + ((ard[4] + ard[5]) + (ard[6] + ard[7]))
    rg_out[...] = total[:, :EXPERTS] / jnp.sqrt(F32(SEGLEN * FF))

    for o in range(GROUPS):
        ref = outs.at[:, pl.ds(0, DS)]
        pltpu.make_async_copy(ref, ref, f_r.at[o]).wait()
    dx_out[...] = outs[...]
    for o in range(1, GROUPS):
        r_copy(NT + o - 1).wait_send()

    def drain_final(q, carry):
        @pl.when(q != d)
        def _():
            final(q, True).wait_send()

        return carry

    lax.fori_loop(0, GROUPS, drain_final, 0)


def run_layer(tokens, cotangent, w_gate, w_up, w_down, router):
    vm, dma = pltpu.VMEM, pltpu.SemaphoreType.DMA
    any_spec = pl.BlockSpec(memory_space=pl.ANY)
    vm_spec = pl.BlockSpec(memory_space=pltpu.VMEM)
    n = GROUPS
    stacked = (3, SEGS, FS, DS)
    scratch = [
        vm((2, BLOCK, n * DS), BF16), vm((SEGS, EXPERTS), F32),
        vm((2, n, 2, NZ, 2, BLOCK, DS), BF16),
        vm((3, EXPERTS, FS, DS), BF16), vm(stacked, BF16),
        vm((DS, DS), BF16), vm((DS, DS), BF16),
        vm((n, NX, 3, FS, LANES), BF16), vm((n, NX, 3, FS, LANES), BF16),
        vm((n, NX, 3, ROWS_A, LANES), BF16),
        vm((n, 3, CUT_A, LANES), BF16), vm((n, 3, ROWS_A - CUT_A, LANES), BF16),
        vm((n, 2, 3, ROWS_A, LANES), BF16),
        vm((n, 2, 3, ROWS_B, LANES), BF16), vm((n, 2, 3, FULL_B, LANES), BF16), vm((n, 3, ROWS_B, LANES), BF16),
        vm((n, 2, NZ, 2, BLOCK, DS), F32), vm((n, 2, NZ, BLOCK, DS), F32),
        vm((n, 2, NZ, BLOCK, DS), BF16), vm((n, NZ - 1, 2, BLOCK, DS), BF16),
        vm((OWN, 2, BLOCK, DS), BF16), vm((OWN, 2, BLOCK, DS), BF16), vm((n, BLOCK, DS), BF16),
        vm((BLOCK, n * DS), BF16),
        vm((DS, DS), F32),
        vm((NT, SEGS, LANES), F32), vm((n, SEGS, LANES), F32),
        dma((6,)), dma((n,)), dma((n,)), dma((5, n)), dma((5, n)),
        dma((10, n)), dma((10, n)), dma((10, n)), dma((10, n)),
        dma((5, n)), dma((5, n)), dma((n,)), dma((n,)), dma((2, n)), dma((NT + n - 1,)), dma((NT + n - 1,)),
    ]
    return pl.pallas_call(
        layer_kernel,
        out_shape=(
            jax.ShapeDtypeStruct((BLOCK, n * DS), BF16),
            jax.ShapeDtypeStruct((SEGS, EXPERTS), F32),
            jax.ShapeDtypeStruct(stacked, BF16),
        ),
        in_specs=[any_spec] * 6,
        out_specs=[vm_spec, vm_spec, any_spec],
        scratch_shapes=scratch,
        compiler_params=pltpu.CompilerParams(
            collective_id=0, has_side_effects=True, vmem_limit_bytes=63 * 2**20
        ),
        name="layer_backward",
    )(tokens, cotangent, router, w_gate, w_up, w_down)


def combine_kernel(router, src, dx_in, rg_in, gate, up, down, dx_out, rg_out, got, made, khi, klo, in_sem, out_sem, pass_sem):
    rows = FS // HALVES
    chunks = [(i, pl.ds(j * rows, rows)) for i in range(3) for j in range(HALVES)]
    ins = [pltpu.make_async_copy(src.at[i, :, at], got.at[n], in_sem.at[n]) for n, (i, at) in enumerate(chunks)]
    outs = [
        pltpu.make_async_copy(made.at[n], (gate, up, down)[i].at[:, at], out_sem.at[n])
        for n, (i, at) in enumerate(chunks)
    ]
    passed = [
        pltpu.make_async_copy(dx_in, dx_out, pass_sem.at[0]),
        pltpu.make_async_copy(rg_in, rg_out, pass_sem.at[1]),
    ]
    for copy in ins + passed:
        copy.start()
    khi[...], klo[...] = spread_coeffs(router[...], by_expert=True)
    for n in range(len(chunks)):
        ins[n].wait()

        def step(r, carry, n=n):
            at = pl.ds(pl.multiple_of(r * PACK, PACK), PACK)
            rhs = got[n, :, at, :].reshape(SEGS * PACK, DS)
            both = nn(khi[...], rhs) + nn(klo[...], rhs)
            made[n, :, at, :] = both.astype(BF16).reshape(EXPERTS, PACK, DS)
            return carry

        lax.fori_loop(0, rows // PACK, step, 0, unroll=11)
        outs[n].start()
    for copy in outs + passed:
        copy.wait()


def combine(router, grads, grad_tokens, router_grad):
    any_spec = pl.BlockSpec(memory_space=pl.ANY)
    n = 3 * HALVES
    like = lambda a: jax.ShapeDtypeStruct(a.shape, a.dtype)
    return pl.pallas_call(
        combine_kernel,
        out_shape=[jax.ShapeDtypeStruct((EXPERTS, FS, DS), BF16)] * 3 + [like(grad_tokens), like(router_grad)],
        in_specs=[pl.BlockSpec(memory_space=pltpu.VMEM)] + [any_spec] * 3,
        out_specs=[any_spec] * 5,
        scratch_shapes=[pltpu.VMEM((n, SEGS, FS // HALVES, DS), BF16)] * 2
        + [pltpu.VMEM((DS, DS), BF16)] * 2
        + [pltpu.SemaphoreType.DMA((n,)), pltpu.SemaphoreType.DMA((n,)), pltpu.SemaphoreType.DMA((2,))],
        compiler_params=pltpu.CompilerParams(vmem_limit_bytes=60 * 2**20),
        name="combine_experts",
    )(router, grads, grad_tokens, router_grad)


def body(tokens, cotangent, w_gate, w_up, w_down, router):
    flip = lambda a: jnp.swapaxes(a, 1, 2)
    grad_tokens, router_grad, grads = run_layer(
        tokens, cotangent, flip(w_gate), flip(w_up), w_down, router
    )
    grad_gate, grad_up, grad_down, grad_tokens, router_grad = combine(router, grads, grad_tokens, router_grad)
    return (grad_tokens, flip(grad_gate), flip(grad_up), grad_down, router_grad)


def solution(mesh):
    placed = (
        P(("dp", "tensor"), None),
        P(("dp", "tensor"), None),
        P(None, "dp", "tensor"),
        P(None, "dp", "tensor"),
        P(None, "tensor", "dp"),
        P(),
    )
    return jax.shard_map(
        body,
        mesh=mesh,
        in_specs=placed,
        out_specs=(
            P(("dp", "tensor"), None),
            P(None, "dp", "tensor"),
            P(None, "dp", "tensor"),
            P(None, "tensor", "dp"),
            P(),
        ),
        check_vma=False,
    )
```

```python
import functools

import jax
import jax.numpy as jnp
from jax import lax
from jax.experimental import pallas as pl
from jax.experimental.pallas import tpu as pltpu
from jax.sharding import PartitionSpec as P

FF = 5632
SEGLEN = 256
MESH = pl.DeviceIdType.MESH
F32 = jnp.float32
BF16 = jnp.bfloat16
NX = 4
NZ = 4
NT = 16
HALVES = 2
GROUPS = 8
OWN = 4
SEGS = 16
EXPERTS = 16
DS = 256
FS = 352
LANES = 128
ROWS_A = 80
ROWS_B = 96
CUT_A = 48
BASE_B = 2 * ROWS_A
FULL_B = 2 * ROWS_B
BACK_A = 64
BACK_B = 112
SWAP = ROWS_A - BACK_A
CUT_BACK = 32
BASE_BACK = 2 * BACK_A
FULL_BACK = 2 * BACK_B
PLACES = (
    (0, 0, BACK_A),
    (BACK_A, BASE_BACK, SWAP),
    (ROWS_A, BACK_A, BACK_A),
    (ROWS_A + BACK_A, BASE_BACK + BACK_B, SWAP),
    (BASE_B, BASE_BACK + SWAP, ROWS_B),
    (BASE_B + ROWS_B, BASE_BACK + BACK_B + SWAP, ROWS_B),
)
BLOCK = 32
PACK = 16

ORDER = (
    ("b3", 6),
    ("a2", 3),
    ("grads", 13),
    ("forward", 0),
    ("spread", -1),
    ("a6", 11),
    ("a5", 10),
    ("eb", 8),
    ("b2", 1),
    ("ea", 8),
    ("b5", 10),
    ("a3", 4),
    ("b6", 11),
    ("d2", 14),
    ("d3", 15),
    ("d4", 16),
    ("settle", 16),
)
LAST = 13
TICKS = GROUPS + LAST


def nn(a, b):
    return jnp.dot(a, b, preferred_element_type=F32)


def dims(a, b, ca, cb):
    return lax.dot_general(a, b, (((ca,), (cb,)), ((), ())), preferred_element_type=F32)


def spread_coeffs(router, by_expert=False):
    wide = (SEGS * PACK, EXPERTS)
    rows = jnp.where(
        lax.broadcasted_iota(jnp.int32, wide, 0) // PACK == lax.broadcasted_iota(jnp.int32, wide, 1), 1.0, 0.0
    )
    exact = dict(precision=lax.Precision.HIGHEST, preferred_element_type=F32)
    tall = lax.dot_general(rows, router, (((1,), (int(by_expert),)), ((), ())), **exact)
    big = lax.dot_general(tall, rows, (((1,), (1,)), ((), ())), **exact)
    row = lax.broadcasted_iota(jnp.int32, big.shape, 0)
    col = lax.broadcasted_iota(jnp.int32, big.shape, 1)
    own = jnp.where((row % PACK) == (col % PACK), big, 0.0)
    hi = own.astype(BF16)
    lo = (own - hi.astype(F32)).astype(BF16)
    return hi, lo


def layer_kernel(
    tok_in, cot_in, router_in, wg_in, wu_in, wd_in,
    dx_out, rg_out, grad_out,
    rows_in, router, x, w, m, khi, klo,
    p, h, ra1, ra2a, ra2b, ra3, rb1, rb2, rb3,
    dx, dxc, dz, rz, dy, ry, fo, outs,
    gsum, art, ard,
    w_sem, t1_s, t1_r, t2_s, t2_r,
    a_s, a_r, b_s, b_r, d_s, d_r, f_s, f_r, pw, r_s, r_r,
):
    d = lax.axis_index("dp")
    t = lax.axis_index("tensor")
    xi, k = d // 2, d % 2
    yh, z, c = t // 8, (t // 2) % NZ, t % 2
    across = (xi * 2 + 1 - k, t)
    high = (d, (1 - yh) * 8 + z * 2 + c)
    twin = (d, yh * 8 + z * 2 + 1 - c)
    xo = lax.rem(xi + 2, NX)

    def sides(q):
        turn = 2 * lax.rem(q, 2)
        xp, xm = lax.rem(xi + 1 + turn, NX), lax.rem(xi + 3 + turn, NX)
        return (xp * 2 + k, t), (xm * 2 + k, t), xp, xm

    def along_z(o):
        return (d, yh * 8 + lax.rem(z + o, NZ) * 2 + c)

    def along_t(o):
        return (d, lax.rem(t + o, NT))

    def along_dp(o):
        return (lax.rem(d + o, GROUPS), t)

    def remote(src, dst, ss, rs, dev):
        return pltpu.make_async_remote_copy(
            src_ref=src, dst_ref=dst, send_sem=ss, recv_sem=rs, device_id=dev, device_id_type=MESH
        )

    loads = [
        pltpu.make_async_copy(src, w.at[i], w_sem.at[i])
        for i, src in enumerate((wg_in, wu_in, wd_in))
    ]
    loads += [
        pltpu.make_async_copy(tok_in, rows_in.at[0], w_sem.at[3]),
        pltpu.make_async_copy(cot_in, rows_in.at[1], w_sem.at[4]),
        pltpu.make_async_copy(router_in, router, w_sem.at[5]),
    ]
    for i in (5, 0, 3, 4, 1, 2):
        loads[i].start()

    peers = [along_dp(o) for o in range(1, GROUPS)] + [along_z(o) for o in range(1, NZ)] + [high, twin]
    barrier = pltpu.get_barrier_semaphore()
    for peer in peers:
        pl.semaphore_signal(barrier, inc=1, device_id=peer, device_id_type=MESH)

    def t1_copy(o):
        dest = lax.rem(d + o, GROUPS)
        cols = pl.ds(pl.multiple_of(dest * DS, LANES), DS)
        src, dst = rows_in.at[:, :, cols], x.at[:, d, yh, z, c]
        if o == 0:
            return pltpu.make_async_copy(src, dst, t1_r.at[0])
        return remote(src, dst, t1_s.at[o], t1_r.at[o], (dest, t))

    loads[5].wait()
    khi[...], klo[...] = spread_coeffs(router[...])

    def merge(i):
        def step(r, carry):
            at = pl.ds(pl.multiple_of(r * PACK, PACK), PACK)
            rhs = w[i, :, at, :].reshape(EXPERTS * PACK, DS)
            both = nn(khi[...], rhs) + nn(klo[...], rhs)
            m[i, :, at, :] = both.astype(BF16).reshape(SEGS, PACK, DS)
            return carry

        lax.fori_loop(0, FS // PACK, step, 0, unroll=11)

    loads[0].wait()
    merge(0)
    pl.semaphore_wait(barrier, len(peers))
    loads[3].wait()
    loads[4].wait()
    for o in (4, 3, 5, 2, 6, 1, 7, 0):
        t1_copy(o).start()
    for i in (1, 2):
        loads[i].wait()
        merge(i)

    def group(q):
        return 2 * lax.rem(q, OWN), lax.rem(yh + q // OWN, 2)

    def segment(q, i):
        first, which = group(q)
        return 2 * (first + i) + which

    def t2_high(a):
        ref = x.at[:, pl.ds(2 * a, 2), yh, z, c]
        return remote(ref, ref, t2_s.at[0, a], t2_r.at[0, a], high)

    def t2_z(q, o):
        first, which = group(q)
        ref = x.at[:, pl.ds(first, 2), which, z, c]
        return remote(ref, ref, t2_s.at[o, q], t2_r.at[o, q], along_z(o))

    def t2_twin(q):
        first, which = group(q)
        ref = x.at[:, pl.ds(first, 2), which, :, c]
        return remote(ref, ref, t2_s.at[4, q], t2_r.at[4, q], twin)

    def hand_on(a, carry):
        for i in range(2):
            o = lax.rem(d - 2 * a - i + GROUPS, GROUPS)
            ref = x.at[:, 2 * a + i, yh, z, c]
            pltpu.make_async_copy(ref, ref, t1_r.at[o]).wait()
        for o in (2, 1, 3):
            t2_z(a, o).start()
        t2_high(a).start()
        return carry

    def hand_on_other(a, carry):
        t2_high(a).wait_recv()
        for o in (2, 1, 3):
            t2_z(OWN + a, o).start()
        return carry

    lax.fori_loop(0, OWN, hand_on, 0)
    lax.fori_loop(0, OWN, hand_on_other, 0)

    mine_a = pl.ds(pl.multiple_of(ROWS_A * k, PACK), ROWS_A)
    mine_a0 = pl.ds(pl.multiple_of(ROWS_A * k, PACK), CUT_A)
    mine_a1 = pl.ds(pl.multiple_of(ROWS_A * k + CUT_A, PACK), ROWS_A - CUT_A)
    theirs_a = pl.ds(pl.multiple_of(ROWS_A * (1 - k), PACK), ROWS_A)
    mine_b = pl.ds(pl.multiple_of(BASE_B + ROWS_B * k, PACK), ROWS_B)
    theirs_b = pl.ds(pl.multiple_of(BASE_B + ROWS_B * (1 - k), PACK), ROWS_B)
    all_b = pl.ds(BASE_B, FULL_B)
    back_a = pl.ds(pl.multiple_of(BACK_A * k, PACK), BACK_A)
    back_a0 = pl.ds(pl.multiple_of(BACK_A * k, PACK), CUT_BACK)
    back_a1 = pl.ds(pl.multiple_of(BACK_A * k + CUT_BACK, PACK), BACK_A - CUT_BACK)
    swap = pl.ds(pl.multiple_of(BASE_BACK + BACK_B * k, PACK), SWAP)
    rest = pl.ds(pl.multiple_of(BASE_BACK + BACK_B * k + SWAP, PACK), ROWS_B)
    back_b = pl.ds(pl.multiple_of(BASE_BACK + BACK_B * k, PACK), BACK_B)
    all_back = pl.ds(BASE_BACK, FULL_BACK)
    back_b0 = pl.ds(BASE_BACK, BACK_B)
    back_b1 = pl.ds(BASE_BACK + BACK_B, BACK_B)
    b0 = pl.ds(BASE_B, ROWS_B)
    b1 = pl.ds(BASE_B + ROWS_B, ROWS_B)

    def a_copy(q, which):
        right, left, xp, xm = sides(q)

        def cp(i, src, dst, dev):
            return remote(src, dst, a_s.at[i, q], a_r.at[i, q], dev)

        same = lambda i, ref, dev: cp(i, ref, ref, dev)
        return [
            lambda: cp(0, p.at[q, :, :, theirs_a, :], ra1.at[q], across),
            lambda: cp(1, p.at[q, xo, :, mine_a0, :], ra2a.at[q], right),
            lambda: cp(2, p.at[q, xo, :, mine_a1, :], ra2b.at[q], left),
            lambda: cp(3, p.at[q, xp, :, mine_a, :], ra3.at[q, 0], right),
            lambda: cp(4, p.at[q, xm, :, mine_a, :], ra3.at[q, 1], left),
            lambda: same(5, h.at[q, xi, :, back_a, :], right),
            lambda: same(6, h.at[q, xi, :, back_a, :], left),
            lambda: same(7, h.at[q, xm, :, back_a1, :], right),
            lambda: same(8, h.at[q, xp, :, back_a0, :], left),
            lambda: same(9, h.at[q, :, :, back_a, :], across),
        ][which]()

    def b_copy(q, which):
        right, left, xp, xm = sides(q)

        def cp(i, src, dst, dev):
            return remote(src, dst, b_s.at[i, q], b_r.at[i, q], dev)

        same = lambda i, ref, dev: cp(i, ref, ref, dev)
        return [
            lambda: cp(0, p.at[q, xo, :, b0, :], rb1.at[q, 0], right),
            lambda: cp(1, p.at[q, xo, :, b1, :], rb1.at[q, 1], left),
            lambda: cp(2, p.at[q, xp, :, all_b, :], rb2.at[q, 0], right),
            lambda: cp(3, p.at[q, xm, :, all_b, :], rb2.at[q, 1], left),
            lambda: cp(4, p.at[q, xi, :, theirs_b, :], rb3.at[q], across),
            lambda: same(5, h.at[q, xi, :, back_b, :], across),
            lambda: same(6, h.at[q, xi, :, all_back, :], right),
            lambda: same(7, h.at[q, xi, :, all_back, :], left),
            lambda: same(8, h.at[q, xm, :, back_b0, :], right),
            lambda: same(9, h.at[q, xp, :, back_b1, :], left),
        ][which]()

    def add(ref, at, other):
        ref[at] = (ref[at].astype(F32) + other.astype(F32)).astype(BF16)

    def matrix(i, q, seg):
        first, which = group(q)
        return x[i, first + seg, which].reshape(SEGLEN, DS)

    def spread(q):
        for o in range(1, NZ):
            t2_z(q, o).wait_recv()
        t2_twin(q).start()

    def forward(q):
        t2_twin(q).wait_recv()
        for seg in range(2):
            s = segment(q, seg)
            xs, dys = matrix(0, q, seg), matrix(1, q, seg)
            for i, rows in enumerate((xs, xs, dys)):
                part = dims(m[i, s], rows, 1, 1).astype(BF16)
                for j in range(2):
                    half = part[:, j * LANES : (j + 1) * LANES]
                    for place, unit, count in PLACES:
                        p[q, 2 * seg + j, i, place : place + count] = half[unit : unit + count]
        a_copy(q, 0).start()
        b_copy(q, 0).start()
        b_copy(q, 1).start()

    def a2(q):
        cps = lambda i: a_copy(q, i)
        cps(0).wait_recv()
        add(p, (q, slice(None), slice(None), mine_a, slice(None)), ra1[q])
        cps(1).start()
        cps(2).start()

    def b2(q):
        xp, xm = sides(q)[2:]
        cps = lambda i: b_copy(q, i)
        cps(0).wait_recv()
        add(p, (q, xp, slice(None), b0, slice(None)), rb1[q, 0])
        cps(2).start()
        cps(1).wait_recv()
        add(p, (q, xm, slice(None), b1, slice(None)), rb1[q, 1])
        cps(3).start()

    def a3(q):
        xp, xm = sides(q)[2:]
        cps = lambda i: a_copy(q, i)
        cps(1).wait_recv()
        add(p, (q, xp, slice(None), mine_a0, slice(None)), ra2a[q])
        cps(3).start()
        cps(2).wait_recv()
        add(p, (q, xm, slice(None), mine_a1, slice(None)), ra2b[q])
        cps(4).start()

    def b3(q):
        cps = lambda i: b_copy(q, i)
        cps(2).wait_recv()
        cps(3).wait_recv()
        at = (q, xi, slice(None), all_b, slice(None))
        p[at] = (p[at].astype(F32) + rb2[q, 0].astype(F32) + rb2[q, 1].astype(F32)).astype(BF16)
        cps(4).start()

    def activate(q, gud, *spans):
        g, u, dh = gud
        sig = jax.nn.sigmoid(g)
        act = g * sig
        made = (dh * u * sig * (1.0 + g * (1.0 - sig)), dh * act, act * u)
        for i, part in enumerate(made):
            first = 0
            for span in spans:
                h[q, xi, i, span, :] = part[first : first + span.size].astype(BF16)
                first += span.size

    def ea(q):
        cps = lambda i: a_copy(q, i)
        cps(3).wait_recv()
        cps(4).wait_recv()
        activate(
            q,
            [
                p[q, xi, i, mine_a, :].astype(F32) + ra3[q, 0, i].astype(F32) + ra3[q, 1, i].astype(F32)
                for i in range(3)
            ],
            back_a,
            swap,
        )
        b_copy(q, 5).start()
        cps(5).start()
        cps(6).start()

    def eb(q):
        cps = lambda i: b_copy(q, i)
        cps(4).wait_recv()
        activate(q, [p[q, xi, i, mine_b, :].astype(F32) + rb3[q, i].astype(F32) for i in range(3)], rest)

    def a5(q):
        cps = lambda i: a_copy(q, i)
        cps(5).wait_recv()
        cps(7).start()
        cps(6).wait_recv()
        cps(8).start()

    def b5(q):
        cps = lambda i: b_copy(q, i)
        cps(5).wait_recv()
        cps(6).start()
        cps(7).start()

    def a6(q):
        cps = lambda i: a_copy(q, i)
        cps(7).wait_recv()
        cps(8).wait_recv()
        cps(9).start()

    def b6(q):
        cps = lambda i: b_copy(q, i)
        cps(6).wait_recv()
        cps(8).start()
        cps(7).wait_recv()
        cps(9).start()

    def keep(q, seg):
        s = segment(q, seg)
        return pltpu.make_async_copy(m.at[:, s], grad_out.at[:, s], pw.at[seg, q])

    def d_copy(q, i):
        def cp(src, dst, dev):
            return remote(src, dst, d_s.at[i, q], d_r.at[i, q], dev)

        if i == 0:
            return cp(dx.at[q, :, :, 1 - c], dxc.at[q], twin)
        if i == 4:
            return remote(dy.at[q], ry.at[q], d_s.at[i, q], d_r.at[i, q], high)
        return cp(dz.at[q, :, lax.rem(z + i, NZ)], rz.at[q, i - 1], along_z(i))

    def grads(q):
        a_copy(q, 9).wait_recv()
        b_copy(q, 8).wait_recv()
        b_copy(q, 9).wait_recv()
        parts = []
        for seg in range(2):
            s = segment(q, seg)
            dg, du, hh = (
                jnp.concatenate([h[q, 2 * seg, i], h[q, 2 * seg + 1, i]], axis=1) for i in range(3)
            )
            dxs = dims(dg, m[0, s], 0, 0) + dims(du, m[1, s], 0, 0)
            dx[q, seg] = dxs.reshape(NZ, 2, BLOCK, DS)
            parts.append((dg, du, hh))
        d_copy(q, 0).start()
        for seg in range(2):
            s = segment(q, seg)
            dg, du, hh = parts[seg]
            xs, dys = matrix(0, q, seg), matrix(1, q, seg)
            m[0, s] = nn(dg, xs).astype(BF16)
            m[1, s] = nn(du, xs).astype(BF16)
            m[2, s] = nn(hh, dys).astype(BF16)
            keep(q, seg).start()

    def d2(q):
        cps = lambda i: d_copy(q, i)
        cps(0).wait_recv()
        total = dx[q, :, :, c] + dxc[q]
        dx[q, :, :, c] = total
        dz[q] = total.astype(BF16)
        for o in range(1, NZ):
            cps(o).start()

    def d3(q):
        cps = lambda i: d_copy(q, i)
        for o in range(1, NZ):
            cps(o).wait_recv()

        total = dx[q, :, z, c]
        for o in range(NZ - 1):
            total = total + rz[q, o].astype(F32)

        @pl.when(q >= OWN)
        def _():
            dy[q - OWN] = total.astype(BF16)
            d_copy(q - OWN, 4).start()

        @pl.when(q < OWN)
        def _():
            dx[q, :, z, c] = total

    def final(dest, away):
        o = lax.rem(dest - d + GROUPS, GROUPS)
        src, dst = fo.at[dest], outs.at[:, pl.ds(pl.multiple_of(d * DS, LANES), DS)]
        if away:
            return remote(src, dst, f_s.at[o], f_r.at[o], (dest, t))
        return pltpu.make_async_copy(src, dst, f_r.at[o])

    def d4(q):
        @pl.when(q >= OWN)
        def _():
            a = q - OWN
            d_copy(a, 4).wait_recv()
            for i in range(2):
                dest = 2 * a + i
                fo[dest] = (dx[a, i, z, c] + ry[a, i].astype(F32)).astype(BF16)

                @pl.when(dest != d)
                def _(dest=dest):
                    final(dest, True).start()

                @pl.when(dest == d)
                def _(dest=dest):
                    final(dest, False).start()

    def settle(q):
        for i in range(10):
            a_copy(q, i).wait_send()
            b_copy(q, i).wait_send()
        for o in range(1, NZ):
            t2_z(q, o).wait_send()
            d_copy(q, o).wait_send()
        t2_twin(q).wait_send()
        d_copy(q, 0).wait_send()
        for seg in range(2):
            keep(q, seg).wait()

    stages = dict(
        settle=settle,
        spread=spread, forward=forward, a2=a2, b2=b2, a3=a3, b3=b3, ea=ea, eb=eb, a5=a5, b5=b5,
        a6=a6, b6=b6, grads=grads, d2=d2, d3=d3, d4=d4,
    )
    spread(0)

    def tick(n, carry):
        for name, lag in ORDER:
            q = n - lag

            @pl.when((q >= (1 if lag < 0 else 0)) & (q < GROUPS))
            def _(name=name, q=q):
                stages[name](q)

        return carry

    lax.fori_loop(0, TICKS, tick, 0)

    gsum[...] = jnp.zeros_like(gsum)

    def inner(i):
        def step(r, carry):
            at = pl.ds(pl.multiple_of(r * PACK, PACK), PACK)
            gsum[...] += dims(
                m[i, :, at, :].reshape(SEGS * PACK, DS), w[i, :, at, :].reshape(EXPERTS * PACK, DS), 1, 1
            )
            return carry

        lax.fori_loop(0, FS // PACK, step, 0, unroll=11)

    last = jnp.int32(GROUPS - 1)
    inner(0)
    d2(last)
    d3(last - 1)
    d4(last - 2)
    inner(1)
    inner(2)
    square = gsum.shape
    row = lax.broadcasted_iota(jnp.int32, square, 0)
    col = lax.broadcasted_iota(jnp.int32, square, 1)
    diag = jnp.where((row % PACK) == (col % PACK), gsum[...], 0.0)
    by_seg = jnp.sum(diag.reshape(SEGS, PACK, EXPERTS * PACK), axis=1)
    pick_row = lax.broadcasted_iota(jnp.int32, (EXPERTS * PACK, LANES), 0)
    pick_col = lax.broadcasted_iota(jnp.int32, (EXPERTS * PACK, LANES), 1)
    pick = jnp.where((pick_row // PACK) == pick_col, 1.0, 0.0).astype(F32)
    own = jnp.dot(by_seg, pick, precision=lax.Precision.HIGHEST, preferred_element_type=F32)

    def r_copy(i):
        def cp(ref, dev):
            return remote(ref, ref, r_s.at[i], r_r.at[i], dev)

        if i < NT:
            return cp(art.at[t], along_t(i))
        return cp(ard.at[d], along_dp(i - NT + 1))

    art[t] = own
    for o in range(1, NT):
        r_copy(o).start()
    d3(last)
    d4(last - 1)

    for o in range(1, NT):
        r_copy(o).wait_recv()
    ard[d] = jnp.sum(art[...], axis=0)
    for o in range(1, GROUPS):
        r_copy(NT + o - 1).start()
    d4(last)

    lax.fori_loop(GROUPS - 3, GROUPS, lambda q, carry: settle(q) or carry, 0)
    for a in range(OWN):
        t2_high(a).wait_send()
        d_copy(a, 4).wait_send()
    for o in range(1, GROUPS):
        t1_copy(o).wait_send()
    for o in range(1, NT):
        r_copy(o).wait_send()
    for o in range(1, GROUPS):
        r_copy(NT + o - 1).wait_recv()
    total = ((ard[0] + ard[1]) + (ard[2] + ard[3])) + ((ard[4] + ard[5]) + (ard[6] + ard[7]))
    rg_out[...] = total[:, :EXPERTS] / jnp.sqrt(F32(SEGLEN * FF))

    for o in range(GROUPS):
        ref = outs.at[:, pl.ds(0, DS)]
        pltpu.make_async_copy(ref, ref, f_r.at[o]).wait()
    dx_out[...] = outs[...]
    for o in range(1, GROUPS):
        r_copy(NT + o - 1).wait_send()

    def drain_final(q, carry):
        @pl.when(q != d)
        def _():
            final(q, True).wait_send()

        return carry

    lax.fori_loop(0, GROUPS, drain_final, 0)


def run_layer(tokens, cotangent, w_gate, w_up, w_down, router):
    vm, dma = pltpu.VMEM, pltpu.SemaphoreType.DMA
    any_spec = pl.BlockSpec(memory_space=pl.ANY)
    vm_spec = pl.BlockSpec(memory_space=pltpu.VMEM)
    n = GROUPS
    stacked = (3, SEGS, FS, DS)
    scratch = [
        vm((2, BLOCK, n * DS), BF16), vm((SEGS, EXPERTS), F32),
        vm((2, n, 2, NZ, 2, BLOCK, DS), BF16),
        vm((3, EXPERTS, FS, DS), BF16), vm(stacked, BF16),
        vm((DS, DS), BF16), vm((DS, DS), BF16),
        vm((n, NX, 3, FS, LANES), BF16), vm((n, NX, 3, FS, LANES), BF16),
        vm((n, NX, 3, ROWS_A, LANES), BF16),
        vm((n, 3, CUT_A, LANES), BF16), vm((n, 3, ROWS_A - CUT_A, LANES), BF16),
        vm((n, 2, 3, ROWS_A, LANES), BF16),
        vm((n, 2, 3, ROWS_B, LANES), BF16), vm((n, 2, 3, FULL_B, LANES), BF16), vm((n, 3, ROWS_B, LANES), BF16),
        vm((n, 2, NZ, 2, BLOCK, DS), F32), vm((n, 2, NZ, BLOCK, DS), F32),
        vm((n, 2, NZ, BLOCK, DS), BF16), vm((n, NZ - 1, 2, BLOCK, DS), BF16),
        vm((OWN, 2, BLOCK, DS), BF16), vm((OWN, 2, BLOCK, DS), BF16), vm((n, BLOCK, DS), BF16),
        vm((BLOCK, n * DS), BF16),
        vm((DS, DS), F32),
        vm((NT, SEGS, LANES), F32), vm((n, SEGS, LANES), F32),
        dma((6,)), dma((n,)), dma((n,)), dma((5, n)), dma((5, n)),
        dma((10, n)), dma((10, n)), dma((10, n)), dma((10, n)),
        dma((5, n)), dma((5, n)), dma((n,)), dma((n,)), dma((2, n)), dma((NT + n - 1,)), dma((NT + n - 1,)),
    ]
    return pl.pallas_call(
        layer_kernel,
        out_shape=(
            jax.ShapeDtypeStruct((BLOCK, n * DS), BF16),
            jax.ShapeDtypeStruct((SEGS, EXPERTS), F32),
            jax.ShapeDtypeStruct(stacked, BF16),
        ),
        in_specs=[any_spec] * 6,
        out_specs=[vm_spec, vm_spec, any_spec],
        scratch_shapes=scratch,
        compiler_params=pltpu.CompilerParams(
            collective_id=0, has_side_effects=True, vmem_limit_bytes=63 * 2**20
        ),
        name="layer_backward",
    )(tokens, cotangent, router, w_gate, w_up, w_down)


def combine_kernel(router, src, dx_in, rg_in, gate, up, down, dx_out, rg_out, got, made, khi, klo, in_sem, out_sem, pass_sem):
    rows = FS // HALVES
    chunks = [(i, pl.ds(j * rows, rows)) for i in range(3) for j in range(HALVES)]
    ins = [pltpu.make_async_copy(src.at[i, :, at], got.at[n], in_sem.at[n]) for n, (i, at) in enumerate(chunks)]
    outs = [
        pltpu.make_async_copy(made.at[n], (gate, up, down)[i].at[:, at], out_sem.at[n])
        for n, (i, at) in enumerate(chunks)
    ]
    passed = [
        pltpu.make_async_copy(dx_in, dx_out, pass_sem.at[0]),
        pltpu.make_async_copy(rg_in, rg_out, pass_sem.at[1]),
    ]
    for copy in ins + passed:
        copy.start()
    khi[...], klo[...] = spread_coeffs(router[...], by_expert=True)
    for n in range(len(chunks)):
        ins[n].wait()

        def step(r, carry, n=n):
            at = pl.ds(pl.multiple_of(r * PACK, PACK), PACK)
            rhs = got[n, :, at, :].reshape(SEGS * PACK, DS)
            both = nn(khi[...], rhs) + nn(klo[...], rhs)
            made[n, :, at, :] = both.astype(BF16).reshape(EXPERTS, PACK, DS)
            return carry

        lax.fori_loop(0, rows // PACK, step, 0, unroll=11)
        outs[n].start()
    for copy in outs + passed:
        copy.wait()


def combine(router, grads, grad_tokens, router_grad):
    any_spec = pl.BlockSpec(memory_space=pl.ANY)
    n = 3 * HALVES
    like = lambda a: jax.ShapeDtypeStruct(a.shape, a.dtype)
    return pl.pallas_call(
        combine_kernel,
        out_shape=[jax.ShapeDtypeStruct((EXPERTS, FS, DS), BF16)] * 3 + [like(grad_tokens), like(router_grad)],
        in_specs=[pl.BlockSpec(memory_space=pltpu.VMEM)] + [any_spec] * 3,
        out_specs=[any_spec] * 5,
        scratch_shapes=[pltpu.VMEM((n, SEGS, FS // HALVES, DS), BF16)] * 2
        + [pltpu.VMEM((DS, DS), BF16)] * 2
        + [pltpu.SemaphoreType.DMA((n,)), pltpu.SemaphoreType.DMA((n,)), pltpu.SemaphoreType.DMA((2,))],
        compiler_params=pltpu.CompilerParams(vmem_limit_bytes=60 * 2**20),
        name="combine_experts",
    )(router, grads, grad_tokens, router_grad)


def body(tokens, cotangent, w_gate, w_up, w_down, router):
    flip = lambda a: jnp.swapaxes(a, 1, 2)
    grad_tokens, router_grad, grads = run_layer(
        tokens, cotangent, flip(w_gate), flip(w_up), w_down, router
    )
    grad_gate, grad_up, grad_down, grad_tokens, router_grad = combine(router, grads, grad_tokens, router_grad)
    return (grad_tokens, flip(grad_gate), flip(grad_up), grad_down, router_grad)


def solution(mesh):
    placed = (
        P(("dp", "tensor"), None),
        P(("dp", "tensor"), None),
        P(None, "dp", "tensor"),
        P(None, "dp", "tensor"),
        P(None, "tensor", "dp"),
        P(),
    )
    return jax.shard_map(
        body,
        mesh=mesh,
        in_specs=placed,
        out_specs=(
            P(("dp", "tensor"), None),
            P(None, "dp", "tensor"),
            P(None, "dp", "tensor"),
            P(None, "tensor", "dp"),
            P(),
        ),
        check_vma=False,
    )
```

```python
import functools

import jax
import jax.numpy as jnp
from jax import lax
from jax.experimental import pallas as pl
from jax.experimental.pallas import tpu as pltpu
from jax.sharding import PartitionSpec as P

FF = 5632
SEGLEN = 256
MESH = pl.DeviceIdType.MESH
F32 = jnp.float32
BF16 = jnp.bfloat16
NX = 4
NZ = 4
NT = 16
HALVES = 2
GROUPS = 8
OWN = 4
SEGS = 16
EXPERTS = 16
DS = 256
FS = 352
LANES = 128
ROWS_A = 80
ROWS_B = 96
CUT_A = 48
BASE_B = 2 * ROWS_A
FULL_B = 2 * ROWS_B
BACK_A = 64
BACK_B = 112
SWAP = ROWS_A - BACK_A
CUT_BACK = 32
BASE_BACK = 2 * BACK_A
FULL_BACK = 2 * BACK_B
PLACES = (
    (0, 0, BACK_A),
    (BACK_A, BASE_BACK, SWAP),
    (ROWS_A, BACK_A, BACK_A),
    (ROWS_A + BACK_A, BASE_BACK + BACK_B, SWAP),
    (BASE_B, BASE_BACK + SWAP, ROWS_B),
    (BASE_B + ROWS_B, BASE_BACK + BACK_B + SWAP, ROWS_B),
)
BLOCK = 32
PACK = 16

ORDER = (
    ("b3", 6),
    ("a2", 3),
    ("d2", 14),
    ("d3", 15),
    ("d4", 16),
    ("settle", 16),
    ("grads", 13),
    ("forward", 0),
    ("spread", -1),
    ("a6", 11),
    ("a5", 10),
    ("eb", 8),
    ("b2", 1),
    ("ea", 8),
    ("b5", 10),
    ("a3", 4),
    ("b6", 11),
)
LAST = 13
TICKS = GROUPS + LAST


def nn(a, b):
    return jnp.dot(a, b, preferred_element_type=F32)


def dims(a, b, ca, cb):
    return lax.dot_general(a, b, (((ca,), (cb,)), ((), ())), preferred_element_type=F32)


def spread_coeffs(router, by_expert=False):
    wide = (SEGS * PACK, EXPERTS)
    rows = jnp.where(
        lax.broadcasted_iota(jnp.int32, wide, 0) // PACK == lax.broadcasted_iota(jnp.int32, wide, 1), 1.0, 0.0
    )
    exact = dict(precision=lax.Precision.HIGHEST, preferred_element_type=F32)
    tall = lax.dot_general(rows, router, (((1,), (int(by_expert),)), ((), ())), **exact)
    big = lax.dot_general(tall, rows, (((1,), (1,)), ((), ())), **exact)
    row = lax.broadcasted_iota(jnp.int32, big.shape, 0)
    col = lax.broadcasted_iota(jnp.int32, big.shape, 1)
    own = jnp.where((row % PACK) == (col % PACK), big, 0.0)
    hi = own.astype(BF16)
    lo = (own - hi.astype(F32)).astype(BF16)
    return hi, lo


def layer_kernel(
    tok_in, cot_in, router_in, wg_in, wu_in, wd_in,
    dx_out, rg_out, grad_out,
    rows_in, router, x, w, m, khi, klo,
    p, h, ra1, ra2a, ra2b, ra3, rb1, rb2, rb3,
    dx, dxc, dz, rz, dy, ry, fo, outs,
    gsum, art, ard,
    w_sem, t1_s, t1_r, t2_s, t2_r,
    a_s, a_r, b_s, b_r, d_s, d_r, f_s, f_r, pw, r_s, r_r,
):
    d = lax.axis_index("dp")
    t = lax.axis_index("tensor")
    xi, k = d // 2, d % 2
    yh, z, c = t // 8, (t // 2) % NZ, t % 2
    across = (xi * 2 + 1 - k, t)
    high = (d, (1 - yh) * 8 + z * 2 + c)
    twin = (d, yh * 8 + z * 2 + 1 - c)
    xo = lax.rem(xi + 2, NX)

    def sides(q):
        turn = 2 * lax.rem(q, 2)
        xp, xm = lax.rem(xi + 1 + turn, NX), lax.rem(xi + 3 + turn, NX)
        return (xp * 2 + k, t), (xm * 2 + k, t), xp, xm

    def along_z(o):
        return (d, yh * 8 + lax.rem(z + o, NZ) * 2 + c)

    def along_t(o):
        return (d, lax.rem(t + o, NT))

    def along_dp(o):
        return (lax.rem(d + o, GROUPS), t)

    def remote(src, dst, ss, rs, dev):
        return pltpu.make_async_remote_copy(
            src_ref=src, dst_ref=dst, send_sem=ss, recv_sem=rs, device_id=dev, device_id_type=MESH
        )

    loads = [
        pltpu.make_async_copy(src, w.at[i], w_sem.at[i])
        for i, src in enumerate((wg_in, wu_in, wd_in))
    ]
    loads += [
        pltpu.make_async_copy(tok_in, rows_in.at[0], w_sem.at[3]),
        pltpu.make_async_copy(cot_in, rows_in.at[1], w_sem.at[4]),
        pltpu.make_async_copy(router_in, router, w_sem.at[5]),
    ]
    for i in (5, 0, 3, 4, 1, 2):
        loads[i].start()

    peers = [along_dp(o) for o in range(1, GROUPS)] + [along_z(o) for o in range(1, NZ)] + [high, twin]
    barrier = pltpu.get_barrier_semaphore()
    for peer in peers:
        pl.semaphore_signal(barrier, inc=1, device_id=peer, device_id_type=MESH)

    def t1_copy(o):
        dest = lax.rem(d + o, GROUPS)
        cols = pl.ds(pl.multiple_of(dest * DS, LANES), DS)
        src, dst = rows_in.at[:, :, cols], x.at[:, d, yh, z, c]
        if o == 0:
            return pltpu.make_async_copy(src, dst, t1_r.at[0])
        return remote(src, dst, t1_s.at[o], t1_r.at[o], (dest, t))

    loads[5].wait()
    khi[...], klo[...] = spread_coeffs(router[...])

    def merge(i):
        def step(r, carry):
            at = pl.ds(pl.multiple_of(r * PACK, PACK), PACK)
            rhs = w[i, :, at, :].reshape(EXPERTS * PACK, DS)
            both = nn(khi[...], rhs) + nn(klo[...], rhs)
            m[i, :, at, :] = both.astype(BF16).reshape(SEGS, PACK, DS)
            return carry

        lax.fori_loop(0, FS // PACK, step, 0, unroll=11)

    loads[0].wait()
    merge(0)
    pl.semaphore_wait(barrier, len(peers))
    loads[3].wait()
    loads[4].wait()
    for o in (4, 3, 5, 2, 6, 1, 7, 0):
        t1_copy(o).start()
    for i in (1, 2):
        loads[i].wait()
        merge(i)

    def group(q):
        return 2 * lax.rem(q, OWN), lax.rem(yh + q // OWN, 2)

    def segment(q, i):
        first, which = group(q)
        return 2 * (first + i) + which

    def t2_high(a):
        ref = x.at[:, pl.ds(2 * a, 2), yh, z, c]
        return remote(ref, ref, t2_s.at[0, a], t2_r.at[0, a], high)

    def t2_z(q, o):
        first, which = group(q)
        ref = x.at[:, pl.ds(first, 2), which, z, c]
        return remote(ref, ref, t2_s.at[o, q], t2_r.at[o, q], along_z(o))

    def t2_twin(q):
        first, which = group(q)
        ref = x.at[:, pl.ds(first, 2), which, :, c]
        return remote(ref, ref, t2_s.at[4, q], t2_r.at[4, q], twin)

    def hand_on(a, carry):
        for i in range(2):
            o = lax.rem(d - 2 * a - i + GROUPS, GROUPS)
            ref = x.at[:, 2 * a + i, yh, z, c]
            pltpu.make_async_copy(ref, ref, t1_r.at[o]).wait()
        for o in (2, 1, 3):
            t2_z(a, o).start()
        t2_high(a).start()
        return carry

    def hand_on_other(a, carry):
        t2_high(a).wait_recv()
        for o in (2, 1, 3):
            t2_z(OWN + a, o).start()
        return carry

    lax.fori_loop(0, OWN, hand_on, 0)
    lax.fori_loop(0, OWN, hand_on_other, 0)

    mine_a = pl.ds(pl.multiple_of(ROWS_A * k, PACK), ROWS_A)
    mine_a0 = pl.ds(pl.multiple_of(ROWS_A * k, PACK), CUT_A)
    mine_a1 = pl.ds(pl.multiple_of(ROWS_A * k + CUT_A, PACK), ROWS_A - CUT_A)
    theirs_a = pl.ds(pl.multiple_of(ROWS_A * (1 - k), PACK), ROWS_A)
    mine_b = pl.ds(pl.multiple_of(BASE_B + ROWS_B * k, PACK), ROWS_B)
    theirs_b = pl.ds(pl.multiple_of(BASE_B + ROWS_B * (1 - k), PACK), ROWS_B)
    all_b = pl.ds(BASE_B, FULL_B)
    back_a = pl.ds(pl.multiple_of(BACK_A * k, PACK), BACK_A)
    back_a0 = pl.ds(pl.multiple_of(BACK_A * k, PACK), CUT_BACK)
    back_a1 = pl.ds(pl.multiple_of(BACK_A * k + CUT_BACK, PACK), BACK_A - CUT_BACK)
    swap = pl.ds(pl.multiple_of(BASE_BACK + BACK_B * k, PACK), SWAP)
    rest = pl.ds(pl.multiple_of(BASE_BACK + BACK_B * k + SWAP, PACK), ROWS_B)
    back_b = pl.ds(pl.multiple_of(BASE_BACK + BACK_B * k, PACK), BACK_B)
    all_back = pl.ds(BASE_BACK, FULL_BACK)
    back_b0 = pl.ds(BASE_BACK, BACK_B)
    back_b1 = pl.ds(BASE_BACK + BACK_B, BACK_B)
    b0 = pl.ds(BASE_B, ROWS_B)
    b1 = pl.ds(BASE_B + ROWS_B, ROWS_B)

    def a_copy(q, which):
        right, left, xp, xm = sides(q)

        def cp(i, src, dst, dev):
            return remote(src, dst, a_s.at[i, q], a_r.at[i, q], dev)

        same = lambda i, ref, dev: cp(i, ref, ref, dev)
        return [
            lambda: cp(0, p.at[q, :, :, theirs_a, :], ra1.at[q], across),
            lambda: cp(1, p.at[q, xo, :, mine_a0, :], ra2a.at[q], right),
            lambda: cp(2, p.at[q, xo, :, mine_a1, :], ra2b.at[q], left),
            lambda: cp(3, p.at[q, xp, :, mine_a, :], ra3.at[q, 0], right),
            lambda: cp(4, p.at[q, xm, :, mine_a, :], ra3.at[q, 1], left),
            lambda: same(5, h.at[q, xi, :, back_a, :], right),
            lambda: same(6, h.at[q, xi, :, back_a, :], left),
            lambda: same(7, h.at[q, xm, :, back_a1, :], right),
            lambda: same(8, h.at[q, xp, :, back_a0, :], left),
            lambda: same(9, h.at[q, :, :, back_a, :], across),
        ][which]()

    def b_copy(q, which):
        right, left, xp, xm = sides(q)

        def cp(i, src, dst, dev):
            return remote(src, dst, b_s.at[i, q], b_r.at[i, q], dev)

        same = lambda i, ref, dev: cp(i, ref, ref, dev)
        return [
            lambda: cp(0, p.at[q, xo, :, b0, :], rb1.at[q, 0], right),
            lambda: cp(1, p.at[q, xo, :, b1, :], rb1.at[q, 1], left),
            lambda: cp(2, p.at[q, xp, :, all_b, :], rb2.at[q, 0], right),
            lambda: cp(3, p.at[q, xm, :, all_b, :], rb2.at[q, 1], left),
            lambda: cp(4, p.at[q, xi, :, theirs_b, :], rb3.at[q], across),
            lambda: same(5, h.at[q, xi, :, back_b, :], across),
            lambda: same(6, h.at[q, xi, :, all_back, :], right),
            lambda: same(7, h.at[q, xi, :, all_back, :], left),
            lambda: same(8, h.at[q, xm, :, back_b0, :], right),
            lambda: same(9, h.at[q, xp, :, back_b1, :], left),
        ][which]()

    def add(ref, at, other):
        ref[at] = (ref[at].astype(F32) + other.astype(F32)).astype(BF16)

    def matrix(i, q, seg):
        first, which = group(q)
        return x[i, first + seg, which].reshape(SEGLEN, DS)

    def spread(q):
        for o in range(1, NZ):
            t2_z(q, o).wait_recv()
        t2_twin(q).start()

    def forward(q):
        t2_twin(q).wait_recv()
        for seg in range(2):
            s = segment(q, seg)
            xs, dys = matrix(0, q, seg), matrix(1, q, seg)
            for i, rows in enumerate((xs, xs, dys)):
                part = dims(m[i, s], rows, 1, 1).astype(BF16)
                for j in range(2):
                    half = part[:, j * LANES : (j + 1) * LANES]
                    for place, unit, count in PLACES:
                        p[q, 2 * seg + j, i, place : place + count] = half[unit : unit + count]
        a_copy(q, 0).start()
        b_copy(q, 0).start()
        b_copy(q, 1).start()

    def a2(q):
        cps = lambda i: a_copy(q, i)
        cps(0).wait_recv()
        add(p, (q, slice(None), slice(None), mine_a, slice(None)), ra1[q])
        cps(1).start()
        cps(2).start()

    def b2(q):
        xp, xm = sides(q)[2:]
        cps = lambda i: b_copy(q, i)
        cps(0).wait_recv()
        add(p, (q, xp, slice(None), b0, slice(None)), rb1[q, 0])
        cps(2).start()
        cps(1).wait_recv()
        add(p, (q, xm, slice(None), b1, slice(None)), rb1[q, 1])
        cps(3).start()

    def a3(q):
        xp, xm = sides(q)[2:]
        cps = lambda i: a_copy(q, i)
        cps(1).wait_recv()
        add(p, (q, xp, slice(None), mine_a0, slice(None)), ra2a[q])
        cps(3).start()
        cps(2).wait_recv()
        add(p, (q, xm, slice(None), mine_a1, slice(None)), ra2b[q])
        cps(4).start()

    def b3(q):
        cps = lambda i: b_copy(q, i)
        cps(2).wait_recv()
        cps(3).wait_recv()
        at = (q, xi, slice(None), all_b, slice(None))
        p[at] = (p[at].astype(F32) + rb2[q, 0].astype(F32) + rb2[q, 1].astype(F32)).astype(BF16)
        cps(4).start()

    def activate(q, gud, *spans):
        g, u, dh = gud
        sig = jax.nn.sigmoid(g)
        act = g * sig
        made = (dh * u * sig * (1.0 + g * (1.0 - sig)), dh * act, act * u)
        for i, part in enumerate(made):
            first = 0
            for span in spans:
                h[q, xi, i, span, :] = part[first : first + span.size].astype(BF16)
                first += span.size

    def ea(q):
        cps = lambda i: a_copy(q, i)
        cps(3).wait_recv()
        cps(4).wait_recv()
        activate(
            q,
            [
                p[q, xi, i, mine_a, :].astype(F32) + ra3[q, 0, i].astype(F32) + ra3[q, 1, i].astype(F32)
                for i in range(3)
            ],
            back_a,
            swap,
        )
        b_copy(q, 5).start()
        cps(5).start()
        cps(6).start()

    def eb(q):
        cps = lambda i: b_copy(q, i)
        cps(4).wait_recv()
        activate(q, [p[q, xi, i, mine_b, :].astype(F32) + rb3[q, i].astype(F32) for i in range(3)], rest)

    def a5(q):
        cps = lambda i: a_copy(q, i)
        cps(5).wait_recv()
        cps(7).start()
        cps(6).wait_recv()
        cps(8).start()

    def b5(q):
        cps = lambda i: b_copy(q, i)
        cps(5).wait_recv()
        cps(6).start()
        cps(7).start()

    def a6(q):
        cps = lambda i: a_copy(q, i)
        cps(7).wait_recv()
        cps(8).wait_recv()
        cps(9).start()

    def b6(q):
        cps = lambda i: b_copy(q, i)
        cps(6).wait_recv()
        cps(8).start()
        cps(7).wait_recv()
        cps(9).start()

    def keep(q, seg):
        s = segment(q, seg)
        return pltpu.make_async_copy(m.at[:, s], grad_out.at[:, s], pw.at[seg, q])

    def d_copy(q, i):
        def cp(src, dst, dev):
            return remote(src, dst, d_s.at[i, q], d_r.at[i, q], dev)

        if i == 0:
            return cp(dx.at[q, :, :, 1 - c], dxc.at[q], twin)
        if i == 4:
            return remote(dy.at[q], ry.at[q], d_s.at[i, q], d_r.at[i, q], high)
        return cp(dz.at[q, :, lax.rem(z + i, NZ)], rz.at[q, i - 1], along_z(i))

    def grads(q):
        a_copy(q, 9).wait_recv()
        b_copy(q, 8).wait_recv()
        b_copy(q, 9).wait_recv()
        parts = []
        for seg in range(2):
            s = segment(q, seg)
            dg, du, hh = (
                jnp.concatenate([h[q, 2 * seg, i], h[q, 2 * seg + 1, i]], axis=1) for i in range(3)
            )
            dxs = dims(dg, m[0, s], 0, 0) + dims(du, m[1, s], 0, 0)
            dx[q, seg] = dxs.reshape(NZ, 2, BLOCK, DS)
            parts.append((dg, du, hh))
        d_copy(q, 0).start()
        for seg in range(2):
            s = segment(q, seg)
            dg, du, hh = parts[seg]
            xs, dys = matrix(0, q, seg), matrix(1, q, seg)
            m[0, s] = nn(dg, xs).astype(BF16)
            m[1, s] = nn(du, xs).astype(BF16)
            m[2, s] = nn(hh, dys).astype(BF16)
            keep(q, seg).start()

    def d2(q):
        cps = lambda i: d_copy(q, i)
        cps(0).wait_recv()
        total = dx[q, :, :, c] + dxc[q]
        dx[q, :, :, c] = total
        dz[q] = total.astype(BF16)
        for o in range(1, NZ):
            cps(o).start()

    def d3(q):
        cps = lambda i: d_copy(q, i)
        for o in range(1, NZ):
            cps(o).wait_recv()

        total = dx[q, :, z, c]
        for o in range(NZ - 1):
            total = total + rz[q, o].astype(F32)

        @pl.when(q >= OWN)
        def _():
            dy[q - OWN] = total.astype(BF16)
            d_copy(q - OWN, 4).start()

        @pl.when(q < OWN)
        def _():
            dx[q, :, z, c] = total

    def final(dest, away):
        o = lax.rem(dest - d + GROUPS, GROUPS)
        src, dst = fo.at[dest], outs.at[:, pl.ds(pl.multiple_of(d * DS, LANES), DS)]
        if away:
            return remote(src, dst, f_s.at[o], f_r.at[o], (dest, t))
        return pltpu.make_async_copy(src, dst, f_r.at[o])

    def d4(q):
        @pl.when(q >= OWN)
        def _():
            a = q - OWN
            d_copy(a, 4).wait_recv()
            for i in range(2):
                dest = 2 * a + i
                fo[dest] = (dx[a, i, z, c] + ry[a, i].astype(F32)).astype(BF16)

                @pl.when(dest != d)
                def _(dest=dest):
                    final(dest, True).start()

                @pl.when(dest == d)
                def _(dest=dest):
                    final(dest, False).start()

    def settle(q):
        for i in range(10):
            a_copy(q, i).wait_send()
            b_copy(q, i).wait_send()
        for o in range(1, NZ):
            t2_z(q, o).wait_send()
            d_copy(q, o).wait_send()
        t2_twin(q).wait_send()
        d_copy(q, 0).wait_send()
        for seg in range(2):
            keep(q, seg).wait()

    stages = dict(
        settle=settle,
        spread=spread, forward=forward, a2=a2, b2=b2, a3=a3, b3=b3, ea=ea, eb=eb, a5=a5, b5=b5,
        a6=a6, b6=b6, grads=grads, d2=d2, d3=d3, d4=d4,
    )
    spread(0)

    def tick(n, carry):
        for name, lag in ORDER:
            q = n - lag

            @pl.when((q >= (1 if lag < 0 else 0)) & (q < GROUPS))
            def _(name=name, q=q):
                stages[name](q)

        return carry

    lax.fori_loop(0, TICKS, tick, 0)

    gsum[...] = jnp.zeros_like(gsum)

    def inner(i):
        def step(r, carry):
            at = pl.ds(pl.multiple_of(r * PACK, PACK), PACK)
            gsum[...] += dims(
                m[i, :, at, :].reshape(SEGS * PACK, DS), w[i, :, at, :].reshape(EXPERTS * PACK, DS), 1, 1
            )
            return carry

        lax.fori_loop(0, FS // PACK, step, 0, unroll=11)

    last = jnp.int32(GROUPS - 1)
    inner(0)
    d2(last)
    d3(last - 1)
    inner(1)
    d4(last - 2)
    inner(2)
    square = gsum.shape
    row = lax.broadcasted_iota(jnp.int32, square, 0)
    col = lax.broadcasted_iota(jnp.int32, square, 1)
    diag = jnp.where((row % PACK) == (col % PACK), gsum[...], 0.0)
    by_seg = jnp.sum(diag.reshape(SEGS, PACK, EXPERTS * PACK), axis=1)
    pick_row = lax.broadcasted_iota(jnp.int32, (EXPERTS * PACK, LANES), 0)
    pick_col = lax.broadcasted_iota(jnp.int32, (EXPERTS * PACK, LANES), 1)
    pick = jnp.where((pick_row // PACK) == pick_col, 1.0, 0.0).astype(F32)
    own = jnp.dot(by_seg, pick, precision=lax.Precision.HIGHEST, preferred_element_type=F32)

    def r_copy(i):
        def cp(ref, dev):
            return remote(ref, ref, r_s.at[i], r_r.at[i], dev)

        if i < NT:
            return cp(art.at[t], along_t(i))
        return cp(ard.at[d], along_dp(i - NT + 1))

    art[t] = own
    for o in range(1, NT):
        r_copy(o).start()
    d3(last)
    d4(last - 1)

    for o in range(1, NT):
        r_copy(o).wait_recv()
    ard[d] = jnp.sum(art[...], axis=0)
    for o in range(1, GROUPS):
        r_copy(NT + o - 1).start()
    d4(last)

    lax.fori_loop(GROUPS - 3, GROUPS, lambda q, carry: settle(q) or carry, 0)
    for a in range(OWN):
        t2_high(a).wait_send()
        d_copy(a, 4).wait_send()
    for o in range(1, GROUPS):
        t1_copy(o).wait_send()
    for o in range(1, NT):
        r_copy(o).wait_send()
    for o in range(1, GROUPS):
        r_copy(NT + o - 1).wait_recv()
    total = ((ard[0] + ard[1]) + (ard[2] + ard[3])) + ((ard[4] + ard[5]) + (ard[6] + ard[7]))
    rg_out[...] = total[:, :EXPERTS] / jnp.sqrt(F32(SEGLEN * FF))

    for o in range(GROUPS):
        ref = outs.at[:, pl.ds(0, DS)]
        pltpu.make_async_copy(ref, ref, f_r.at[o]).wait()
    dx_out[...] = outs[...]
    for o in range(1, GROUPS):
        r_copy(NT + o - 1).wait_send()

    def drain_final(q, carry):
        @pl.when(q != d)
        def _():
            final(q, True).wait_send()

        return carry

    lax.fori_loop(0, GROUPS, drain_final, 0)


def run_layer(tokens, cotangent, w_gate, w_up, w_down, router):
    vm, dma = pltpu.VMEM, pltpu.SemaphoreType.DMA
    any_spec = pl.BlockSpec(memory_space=pl.ANY)
    vm_spec = pl.BlockSpec(memory_space=pltpu.VMEM)
    n = GROUPS
    stacked = (3, SEGS, FS, DS)
    scratch = [
        vm((2, BLOCK, n * DS), BF16), vm((SEGS, EXPERTS), F32),
        vm((2, n, 2, NZ, 2, BLOCK, DS), BF16),
        vm((3, EXPERTS, FS, DS), BF16), vm(stacked, BF16),
        vm((DS, DS), BF16), vm((DS, DS), BF16),
        vm((n, NX, 3, FS, LANES), BF16), vm((n, NX, 3, FS, LANES), BF16),
        vm((n, NX, 3, ROWS_A, LANES), BF16),
        vm((n, 3, CUT_A, LANES), BF16), vm((n, 3, ROWS_A - CUT_A, LANES), BF16),
        vm((n, 2, 3, ROWS_A, LANES), BF16),
        vm((n, 2, 3, ROWS_B, LANES), BF16), vm((n, 2, 3, FULL_B, LANES), BF16), vm((n, 3, ROWS_B, LANES), BF16),
        vm((n, 2, NZ, 2, BLOCK, DS), F32), vm((n, 2, NZ, BLOCK, DS), F32),
        vm((n, 2, NZ, BLOCK, DS), BF16), vm((n, NZ - 1, 2, BLOCK, DS), BF16),
        vm((OWN, 2, BLOCK, DS), BF16), vm((OWN, 2, BLOCK, DS), BF16), vm((n, BLOCK, DS), BF16),
        vm((BLOCK, n * DS), BF16),
        vm((DS, DS), F32),
        vm((NT, SEGS, LANES), F32), vm((n, SEGS, LANES), F32),
        dma((6,)), dma((n,)), dma((n,)), dma((5, n)), dma((5, n)),
        dma((10, n)), dma((10, n)), dma((10, n)), dma((10, n)),
        dma((5, n)), dma((5, n)), dma((n,)), dma((n,)), dma((2, n)), dma((NT + n - 1,)), dma((NT + n - 1,)),
    ]
    return pl.pallas_call(
        layer_kernel,
        out_shape=(
            jax.ShapeDtypeStruct((BLOCK, n * DS), BF16),
            jax.ShapeDtypeStruct((SEGS, EXPERTS), F32),
            jax.ShapeDtypeStruct(stacked, BF16),
        ),
        in_specs=[any_spec] * 6,
        out_specs=[vm_spec, vm_spec, any_spec],
        scratch_shapes=scratch,
        compiler_params=pltpu.CompilerParams(
            collective_id=0, has_side_effects=True, vmem_limit_bytes=63 * 2**20
        ),
        name="layer_backward",
    )(tokens, cotangent, router, w_gate, w_up, w_down)


def combine_kernel(router, src, dx_in, rg_in, gate, up, down, dx_out, rg_out, got, made, khi, klo, in_sem, out_sem, pass_sem):
    rows = FS // HALVES
    chunks = [(i, pl.ds(j * rows, rows)) for i in range(3) for j in range(HALVES)]
    ins = [pltpu.make_async_copy(src.at[i, :, at], got.at[n], in_sem.at[n]) for n, (i, at) in enumerate(chunks)]
    outs = [
        pltpu.make_async_copy(made.at[n], (gate, up, down)[i].at[:, at], out_sem.at[n])
        for n, (i, at) in enumerate(chunks)
    ]
    passed = [
        pltpu.make_async_copy(dx_in, dx_out, pass_sem.at[0]),
        pltpu.make_async_copy(rg_in, rg_out, pass_sem.at[1]),
    ]
    for copy in ins + passed:
        copy.start()
    khi[...], klo[...] = spread_coeffs(router[...], by_expert=True)
    for n in range(len(chunks)):
        ins[n].wait()

        def step(r, carry, n=n):
            at = pl.ds(pl.multiple_of(r * PACK, PACK), PACK)
            rhs = got[n, :, at, :].reshape(SEGS * PACK, DS)
            both = nn(khi[...], rhs) + nn(klo[...], rhs)
            made[n, :, at, :] = both.astype(BF16).reshape(EXPERTS, PACK, DS)
            return carry

        lax.fori_loop(0, rows // PACK, step, 0, unroll=11)
        outs[n].start()
    for copy in outs + passed:
        copy.wait()


def combine(router, grads, grad_tokens, router_grad):
    any_spec = pl.BlockSpec(memory_space=pl.ANY)
    n = 3 * HALVES
    like = lambda a: jax.ShapeDtypeStruct(a.shape, a.dtype)
    return pl.pallas_call(
        combine_kernel,
        out_shape=[jax.ShapeDtypeStruct((EXPERTS, FS, DS), BF16)] * 3 + [like(grad_tokens), like(router_grad)],
        in_specs=[pl.BlockSpec(memory_space=pltpu.VMEM)] + [any_spec] * 3,
        out_specs=[any_spec] * 5,
        scratch_shapes=[pltpu.VMEM((n, SEGS, FS // HALVES, DS), BF16)] * 2
        + [pltpu.VMEM((DS, DS), BF16)] * 2
        + [pltpu.SemaphoreType.DMA((n,)), pltpu.SemaphoreType.DMA((n,)), pltpu.SemaphoreType.DMA((2,))],
        compiler_params=pltpu.CompilerParams(vmem_limit_bytes=60 * 2**20),
        name="combine_experts",
    )(router, grads, grad_tokens, router_grad)


def body(tokens, cotangent, w_gate, w_up, w_down, router):
    flip = lambda a: jnp.swapaxes(a, 1, 2)
    grad_tokens, router_grad, grads = run_layer(
        tokens, cotangent, flip(w_gate), flip(w_up), w_down, router
    )
    grad_gate, grad_up, grad_down, grad_tokens, router_grad = combine(router, grads, grad_tokens, router_grad)
    return (grad_tokens, flip(grad_gate), flip(grad_up), grad_down, router_grad)


def solution(mesh):
    placed = (
        P(("dp", "tensor"), None),
        P(("dp", "tensor"), None),
        P(None, "dp", "tensor"),
        P(None, "dp", "tensor"),
        P(None, "tensor", "dp"),
        P(),
    )
    return jax.shard_map(
        body,
        mesh=mesh,
        in_specs=placed,
        out_specs=(
            P(("dp", "tensor"), None),
            P(None, "dp", "tensor"),
            P(None, "dp", "tensor"),
            P(None, "tensor", "dp"),
            P(),
        ),
        check_vma=False,
    )
```
